32 devices in a mesh: fsdp: 4 (over x, core), context: 2 (over y), tensor: 4 (over z).
Axes of the slice: x: 2, y: 2, z: 4, core: 2. Of those that a mesh axis runs over, the one named last changes fastest.
Arguments:
- block_in: bfloat16 [2048, 2048], P(('fsdp', 'context')), may hold values from -6 to 6
- seq_lengths: int32 [4, 6], P('fsdp'), may hold values from 0 to 512, as said below
- attn_gain: float32 [2048], replicated, may hold values from 0.25 to 1.75
- attn_bias: float32 [2048], replicated, may hold values from -1.75 to 1.75
- qkv_weight: bfloat16 [3, 2048, 2048], P(None, ('fsdp', 'context'), 'tensor'), may hold values from -0.125 to 0.125
- qkv_bias: float32 [3, 2048], P(None, 'tensor'), may hold values from -3 to 3
- out_weight: bfloat16 [2048, 2048], P('tensor', ('fsdp', 'context')), may hold values from -0.5 to 0.5
- ffn_gain: float32 [2048], replicated, may hold values from 0.25 to 1.75
- ffn_bias: float32 [2048], replicated, may hold values from -1.75 to 1.75
- gate_up_weight: bfloat16 [2, 2048, 5632], P(None, ('fsdp', 'context'), 'tensor'), may hold values from -0.125 to 0.125
- down_weight: bfloat16 [5632, 2048], P('tensor', ('fsdp', 'context')), may hold values from -0.15625 to 0.15625
- out_cotangent: bfloat16 [2048, 2048], P(('fsdp', 'context')), may hold values from -6 to 6
Outputs:
- block_out: bfloat16 [2048, 2048], P(('fsdp', 'context'))
- input_grad: bfloat16 [2048, 2048], P(('fsdp', 'context'))
- attn_gain_grad: float32 [2048], replicated
- attn_bias_grad: float32 [2048], replicated
- qkv_weight_grad: float32 [3, 2048, 2048], P(None, ('fsdp', 'context'), 'tensor')
- qkv_bias_grad: float32 [3, 2048], P(None, 'tensor')
- out_weight_grad: float32 [2048, 2048], P('tensor', ('fsdp', 'context'))
- ffn_gain_grad: float32 [2048], replicated
- ffn_bias_grad: float32 [2048], replicated
- gate_up_grad: float32 [2, 2048, 5632], P(None, ('fsdp', 'context'), 'tensor')
- down_grad: float32 [5632, 2048], P('tensor', ('fsdp', 'context'))
The draws below stay inside these ranges and needn't reach their ends.
Inputs may be any that keep to these rules, and one draw needn't show every extreme that they name: `seq_lengths`: each row sums to 512; in each row one sequence starts before place 256 and ends after it.
All inputs are finite; a program needn't handle non-finite values.
Results may differ from the reference program's by a relative error of at most 0.015.
Values may be sent and summed in bfloat16 or wider, within the bound.
No kernel may reach another device: no remote copies, remote signals or barrier semaphores. Data moves between devices by JAX's collectives and lax.ppermute only.
A program may use at most 256 MiB of HBM per device.

```python
import math
import jax
import jax.numpy as jnp
from jax import lax

D = 2048
HEADS = 32
FF = 5632
TOK_DEV = 256
SEQS = 6
HD = 64
ROT = 16
GROUPS = 4
SEQ_TOK = 512
TOKENS = 2048


def draw_seq_lengths(key, part):
    key = jax.random.fold_in(key, 7)
    subkeys = jax.random.split(key, 5)
    cross_slot = jax.random.randint(subkeys[0], (GROUPS,), 0, SEQS)
    seq_begin = jax.random.randint(subkeys[1], (GROUPS,), 0, TOK_DEV)
    seq_finish = jax.random.randint(subkeys[2], (GROUPS,), TOK_DEV + 1, SEQ_TOK + 1)
    whole_group = jax.random.randint(subkeys[3], (), 0, GROUPS)
    is_whole = jnp.arange(GROUPS) == whole_group
    seq_begin = jnp.where((cross_slot == 0) | is_whole, 0, seq_begin)
    seq_finish = jnp.where((cross_slot == SEQS - 1) | is_whole, SEQ_TOK, seq_finish)
    raw_draw = jax.random.randint(subkeys[4], (GROUPS, SEQS + 1), 0, SEQ_TOK + 1)
    slot_ids = jnp.arange(SEQS + 1)[None, :]
    before_cut = raw_draw * seq_begin[:, None] // SEQ_TOK
    after_cut = seq_finish[:, None] + raw_draw * (SEQ_TOK - seq_finish[:, None]) // SEQ_TOK
    cross_col = cross_slot[:, None]
    bounds = jnp.where(slot_ids < cross_col, before_cut, jnp.where(slot_ids == cross_col, seq_begin[:, None], jnp.where(slot_ids == cross_col + 1, seq_finish[:, None], after_cut)))
    bounds = jnp.where(slot_ids == 0, 0, jnp.where(slot_ids == SEQS, SEQ_TOK, bounds))
    bounds = jnp.sort(bounds, axis=1)
    return (bounds[:, 1:] - bounds[:, :-1]).astype(jnp.int32)


def level_of(key, dims, shards, least, largest):
    level = 1.0
    for position, shards_of in shards:
        draws = jax.random.uniform(jax.random.fold_in(jax.random.fold_in(key, 6), position), (shards_of,), jnp.float32, least / len(shards), largest / len(shards))
        level = level * jnp.repeat(jnp.exp(draws), dims[position] // shards_of).reshape((-1,) + (1,) * (len(dims) - 1 - position))
    return level


def centred(stream_key, dims, deviation, bound, pieces=(), dtype=jnp.bfloat16):
    array = deviation * jax.random.normal(stream_key, dims, jnp.float32)
    if pieces:
        array = array * level_of(stream_key, dims, pieces, -0.22, 0.18)
    return jnp.clip(array, -bound, bound).astype(dtype)


def setup_inputs(seed: int = 0) -> dict:
    seeds = jax.random.split(jax.random.key(seed), 13)
    block_in = centred(seeds[0], (TOKENS, D), 1.0, 6.0, ((0, 8),))
    seq_lengths = draw_seq_lengths(jax.random.fold_in(seeds[12], 71), 0)
    attn_gain = jnp.clip(1.0 + 0.15 * jax.random.normal(seeds[2], (D,), jnp.float32), 0.25, 1.75)
    attn_bias = centred(seeds[3], (D,), 0.3, 1.75, (), jnp.float32)
    qkv_weight = centred(seeds[4], (3, D, D), D ** -0.5, 0.125, ((1, 8), (2, 4)))
    qkv_bias = centred(seeds[5], (3, D), 0.5, 3.0, ((1, 4),), jnp.float32)
    out_weight = centred(seeds[6], (D, D), (D // 16) ** -0.5, 0.5, ((0, 4), (1, 8)))
    ffn_gain = jnp.clip(1.0 + 0.15 * jax.random.normal(seeds[7], (D,), jnp.float32), 0.25, 1.75)
    ffn_bias = centred(seeds[8], (D,), 0.3, 1.75, (), jnp.float32)
    gate_up_weight = centred(seeds[9], (2, D, FF), D ** -0.5, 0.125, ((1, 8), (2, 4)))
    down_weight = centred(seeds[10], (FF, D), (FF // 4) ** -0.5, 0.15625, ((0, 4), (1, 8)))
    out_cotangent = centred(seeds[11], (TOKENS, D), 1.0, 6.0, ((0, 8),))
    return dict(block_in=block_in, seq_lengths=seq_lengths, attn_gain=attn_gain, attn_bias=attn_bias, qkv_weight=qkv_weight, qkv_bias=qkv_bias, out_weight=out_weight, ffn_gain=ffn_gain, ffn_bias=ffn_bias, gate_up_weight=gate_up_weight, down_weight=down_weight, out_cotangent=out_cotangent)


EPS = 1e-05
NEG = -1e+30
HIGH = lax.Precision.HIGHEST

@jax.custom_vjp
def low(v):
    return lax.optimization_barrier(v.astype(jnp.bfloat16)).astype(jnp.float32)

@jax.custom_vjp
def low_back(v):
    return v

def low_keep(v):
    return (low(v), None)

def low_pass(kept, grad):
    return (grad,)

def back_keep(v):
    return (v, None)

def back_low(kept, grad):
    return (low(grad),)
low.defvjp(low_keep, low_pass)
low_back.defvjp(back_keep, back_low)

def layer_norm(values, gain_vec, bias_vec):
    center = values - lax.optimization_barrier(jnp.mean(values, axis=-1, keepdims=True))
    spread = lax.optimization_barrier(jnp.mean(center * center, axis=-1, keepdims=True))
    return center * lax.rsqrt(spread + EPS) * gain_vec + bias_vec

def rotary(values, places):
    half_rot = ROT // 2
    frequency = jnp.exp(jnp.arange(half_rot).astype(jnp.float32) * (-2.0 * math.log(10000.0) / ROT))
    angles = places.astype(jnp.float32)[:, None] * frequency[None, :]
    cosine_table = jnp.cos(angles)[:, None, :]
    sine_table = jnp.sin(angles)[:, None, :]
    first_half = values[..., :half_rot]
    second_half = values[..., half_rot:ROT]
    return jnp.concatenate([first_half * cosine_table - second_half * sine_table, second_half * cosine_table + first_half * sine_table, values[..., ROT:]], axis=-1)

def group_layer(weights, group_in, seg_lengths):
    attn_gain, attn_bias, qkv_weight, qkv_bias, out_weight, ffn_gain, ffn_bias, gate_up_weight, down_weight = weights
    row_count = group_in.shape[0]
    score_scale = HD ** (-0.5)
    places = jnp.arange(row_count).astype(jnp.int32)
    seq_ends = jnp.cumsum(seg_lengths).astype(jnp.int32)
    starts = lax.optimization_barrier(jnp.sum(jnp.where(seq_ends[None, :] <= places[:, None], seg_lengths[None, :], 0), axis=1)).astype(jnp.int32)
    normed_one = low(layer_norm(group_in, attn_gain, attn_bias))
    projected = low_back(jnp.einsum('td,kde->kte', normed_one, qkv_weight, precision=HIGH) + qkv_bias[:, None, :])
    queries = low(rotary(projected[0].reshape(row_count, HEADS, HD), places - starts))
    keys_all = low(rotary(projected[1].reshape(row_count, HEADS, HD), places - starts))
    values_all = low(projected[2].reshape(row_count, HEADS, HD))
    block_rows = min(512, row_count)

    def attend(block_id):
        block_start = block_id * block_rows
        query_blk = lax.dynamic_slice_in_dim(queries, block_start, block_rows, 0)
        query_at = lax.dynamic_slice_in_dim(places, block_start, block_rows, 0)
        query_from = lax.dynamic_slice_in_dim(starts, block_start, block_rows, 0)
        scores = low_back(jnp.einsum('qhd,khd->hqk', query_blk, keys_all, precision=HIGH) * score_scale)
        visible = (places[None, :] <= query_at[:, None]) & (places[None, :] >= query_from[:, None])
        scores = jnp.where(visible[None], scores, NEG)
        row_top = lax.optimization_barrier(jnp.max(scores, axis=-1, keepdims=True))
        exp_scores = jnp.exp(scores - row_top)
        attn_weights = low(exp_scores / lax.optimization_barrier(jnp.sum(exp_scores, axis=-1, keepdims=True)))
        return jnp.einsum('hqk,khd->qhd', attn_weights, values_all, precision=HIGH)
    attended = lax.map(jax.checkpoint(attend), jnp.arange(row_count // block_rows).astype(jnp.int32))
    attended = low(low_back(attended.reshape(row_count, D)))
    residual_mid = group_in + low_back(jnp.dot(attended, out_weight, precision=HIGH))
    normed_two = low(layer_norm(residual_mid, ffn_gain, ffn_bias))
    gate_up = low_back(jnp.einsum('td,kdf->ktf', normed_two, gate_up_weight, precision=HIGH))
    hidden = low(jax.nn.silu(gate_up[0]) * gate_up[1])
    return residual_mid + jnp.dot(hidden, down_weight, precision=HIGH)

def reference(block_in, seq_lengths, attn_gain, attn_bias, qkv_weight, qkv_bias, out_weight, ffn_gain, ffn_bias, gate_up_weight, down_weight, out_cotangent):

    def forward(inputs_f, *weights):

        def step_group(carry, item):
            group_in, seg_lengths = item
            return (carry, jax.checkpoint(group_layer)(weights, group_in, seg_lengths))
        _, group_outs = lax.scan(step_group, jnp.zeros((), jnp.float32), (inputs_f.reshape(GROUPS, SEQ_TOK, D), seq_lengths))
        return group_outs.reshape(TOKENS, D)
    primals = (block_in.astype(jnp.float32), attn_gain, attn_bias, qkv_weight.astype(jnp.float32), qkv_bias, out_weight.astype(jnp.float32), ffn_gain, ffn_bias, gate_up_weight.astype(jnp.float32), down_weight.astype(jnp.float32))
    result, pullback = jax.vjp(forward, *primals)
    grads = pullback(out_cotangent.astype(jnp.float32))
    return (result.astype(jnp.bfloat16), grads[0].astype(jnp.bfloat16), grads[1], grads[2], grads[3], grads[4], grads[5], grads[6], grads[7], grads[8], grads[9])
```

```python
import functools
import math

import jax
import jax.numpy as jnp
from jax import lax
from jax.experimental import pallas as pl
from jax.experimental.pallas import tpu as pltpu
from jax.sharding import PartitionSpec as P

HD = 64
ROT = 16
EPS = 1e-05
NEG = -1e30
f32 = jnp.float32
bf16 = jnp.bfloat16
VM = pl.BlockSpec(memory_space=pltpu.VMEM)
SM = pl.BlockSpec(memory_space=pltpu.SMEM)
PLANE = ("fsdp", "context")


def shape(dims, dtype):
    return jax.ShapeDtypeStruct(tuple(dims), dtype)


def call(kernel, name, outs, args, specs, scratch=(), flops=0, moved=0):
    return pl.pallas_call(
        kernel,
        name=name,
        out_shape=outs,
        in_specs=specs,
        out_specs=jax.tree.map(lambda _: VM, outs),
        scratch_shapes=list(scratch),
        compiler_params=pltpu.CompilerParams(vmem_limit_bytes=56 * 2**20),
        cost_estimate=pl.CostEstimate(flops=flops, bytes_accessed=moved, transcendentals=0),
    )(*args)


def dot(a, b, dims=((1,), (0,))):
    return lax.dot_general(a, b, (dims, ((), ())), preferred_element_type=f32)


NT = ((1,), (1,))
TN = ((0,), (0,))


class Plane:
    def __init__(self):
        self.fsdp = lax.axis_size("fsdp")
        self.context = lax.axis_size("context")
        self.count = self.fsdp * self.context
        self.me = lax.axis_index("fsdp") * self.context + lax.axis_index("context")
        core = self.context
        rest = [1 << i for i in range(int(math.log2(self.count))) if (1 << i) != core]
        self.core = core
        self.orders = (rest[::-1], rest)

    def swap(self, value, bit):
        if bit < self.context:
            pairs = [(i, i ^ bit) for i in range(self.context)]
            return lax.ppermute(value, "context", pairs)
        step = bit // self.context
        pairs = [(i, i ^ step) for i in range(self.fsdp)]
        return lax.ppermute(value, "fsdp", pairs)

    def gather(self, halves):
        slots = [{0: halves[0]}, {0: halves[1]}]
        for step in range(len(self.orders[0]) + 1):
            for h in (0, 1):
                order = self.orders[h] + [self.core]
                bit = order[step]
                for k in list(slots[h]):
                    slots[h][k ^ bit] = self.swap(slots[h][k], bit)
        return slots

    def scatter(self, slots):
        slots = [dict(slots[0]), dict(slots[1])]
        for step in range(len(self.orders[0]) + 1):
            last = step == len(self.orders[0])
            for h in (0, 1):
                order = [self.core] + self.orders[h]
                bit = order[step]
                sent = {k: self.swap(v, bit) for k, v in slots[h].items() if k & bit}
                kept = {}
                for k, v in slots[h].items():
                    if not k & bit:
                        total = v.astype(f32) + sent[k ^ bit].astype(f32)
                        kept[k] = total if last else total.astype(bf16)
                slots[h] = kept
        return slots[0][0], slots[1][0]

    def total(self, value, over_tensor):
        value = value + 0.0
        bit = 1
        while bit < self.count:
            value = value + self.swap(value, bit)
            bit *= 2
        if over_tensor:
            value = value + sum(tensor_swap(value, j) for j in range(1, lax.axis_size("tensor")))
        return value


def tensor_swap(value, j):
    peers = lax.axis_size("tensor")
    return lax.ppermute(value, "tensor", [(i, i ^ j) for i in range(peers)])


def tensor_exchange(parts):
    return [tensor_swap(part, j) for j, part in enumerate(parts) if j]


def tensor_gather(part):
    return [part] + [tensor_swap(part, j) for j in range(1, lax.axis_size("tensor"))]


def row_stats(x3):
    size = x3.shape[0] * x3.shape[2]
    mean = jnp.sum(jnp.sum(x3, axis=0), axis=-1, keepdims=True) / size
    center = x3 - mean[None]
    var = jnp.sum(jnp.sum(center * center, axis=0), axis=-1, keepdims=True) / size
    inv = lax.rsqrt(var + EPS)
    return center * inv[None], inv


def row_mean(x3):
    return jnp.sum(jnp.sum(x3, axis=0), axis=-1, keepdims=True) / (x3.shape[0] * x3.shape[2])


def split(x, count):
    width = x.shape[1] // count
    return jnp.stack([x[:, i * width : (i + 1) * width] for i in range(count)])


def norm_kernel(x_ref, gain_ref, bias_ref, out_ref):
    normal, _ = row_stats(split(x_ref[...].astype(f32), out_ref.shape[0]))
    out_ref[...] = (normal * gain_ref[...] + bias_ref[...]).astype(bf16)


def reorder_kernel(at_ref, x_ref, out_ref):
    rows = x_ref.shape[0] // at_ref.shape[0]
    for j in range(at_ref.shape[0]):
        block = x_ref[pl.ds(pl.multiple_of(at_ref[j] * rows, rows), rows), :]
        out_ref[:, j * rows : (j + 1) * rows, :] = split(block, out_ref.shape[0])


def spin(x, tables, sign):
    parts = []
    for i in range(x.shape[1] // 128):
        v = x[:, i * 128 : (i + 1) * 128]
        turned = pltpu.roll(v, 128 - ROT // 2, 1) * tables[1] + pltpu.roll(v, ROT // 2, 1) * tables[2]
        parts.append(v * tables[0] + (turned if sign > 0 else -turned))
    return jnp.concatenate(parts, axis=1)


def qkv_kernel(count, order_ref, normed_ref, bias_ref, table_ref, *refs):
    weights = refs[: 2 * count]
    q_ref, kv_ref = refs[2 * count :]
    width = q_ref.shape[1] // 2
    for h in range(2):
        cols = slice(h * width, (h + 1) * width)
        for j in range(3):
            total = bias_ref[j, :, cols]
            for k in range(count):
                total = total + dot(normed_ref[order_ref[k]], weights[h * count + k][j])
            if j < 2:
                total = spin(total, table_ref[...], 1)
            if j == 0:
                q_ref[:, cols] = total.astype(bf16)
            else:
                kv_ref[j - 1, :, cols] = total.astype(bf16)


def head_mask(rows, h):
    lane = lax.broadcasted_iota(jnp.int32, (rows, 2 * HD), 1)
    return (lane // HD) == h


def attend_kernel(count, order_ref, at_ref, hide_ref, q_ref, here_ref, early_ref, *refs):
    weights = refs[: 2 * count]
    att_ref, log_ref, own_ref = refs[2 * count : 2 * count + 3]
    sends = refs[2 * count + 3 : -1]
    part_ref = refs[-1]
    rows, feat = q_ref.shape
    scale = HD**-0.5
    for pair in range(feat // (2 * HD)):
        cols = slice(pair * 2 * HD, (pair + 1) * 2 * HD)
        q = q_ref[:, cols]
        k = jnp.concatenate([early_ref[0, :, cols], here_ref[0, :, cols]], axis=0)
        v = jnp.concatenate([early_ref[1, :, cols], here_ref[1, :, cols]], axis=0)
        out = []
        for h in range(2):
            mask = head_mask(rows, h)
            scores = dot(jnp.where(mask, q, 0), k, NT) * scale + hide_ref[...]
            top = jnp.max(scores, axis=-1, keepdims=True)
            exps = jnp.exp(scores - top)
            total = jnp.sum(exps, axis=-1, keepdims=True)
            log_ref[2 * pair + h] = top + jnp.log(total)
            out.append(dot((exps / total).astype(bf16), v))
        att_ref[:, cols] = jnp.where(head_mask(rows, 0), out[0], out[1]).astype(bf16)
    half = feat // 2
    for k in range(count):
        part_ref[order_ref[k]] = dot(att_ref[:, :half], weights[k][...]) + dot(
            att_ref[:, half:], weights[count + k][...]
        )
    hand_out(at_ref, part_ref, own_ref, sends)


def hand_out(at_ref, part_ref, own_ref, sends):
    rows = own_ref.shape[1]
    for j in range(at_ref.shape[0]):
        block = part_ref[:, pl.ds(pl.multiple_of(at_ref[j] * rows, rows), rows), :]
        if j == 0:
            own_ref[...] = block
        else:
            sends[j - 1][...] = block.astype(bf16)


def mid_kernel(at_ref, x_ref, gain_ref, bias_ref, own_ref, *refs):
    mid_ref, normed_ref = refs[-2:]
    rows = own_ref.shape[1]
    total = own_ref[...]
    for ref in refs[:-2]:
        total = total + ref[...].astype(f32)
    block = x_ref[pl.ds(pl.multiple_of(at_ref[0] * rows, rows), rows), :].astype(f32)
    mid = split(block, own_ref.shape[0]) + total
    mid_ref[...] = mid
    normal, _ = row_stats(mid)
    normed_ref[...] = (normal * gain_ref[...] + bias_ref[...]).astype(bf16)


def stacked(refs):
    return jnp.concatenate([ref[0] for ref in refs], axis=0)


def ffn_kernel(peers, *refs):
    blocks = refs[:peers]
    cot_ref, w_ref, hidden_ref, gate_grad_ref, up_grad_ref, gate, up, back = refs[peers:]
    step = pl.program_id(0)
    width = cot_ref.shape[2]
    x = stacked(blocks)

    @pl.when(step == 0)
    def _():
        gate[...] = jnp.zeros_like(gate)
        up[...] = jnp.zeros_like(up)
        back[...] = jnp.zeros_like(back)

    gate[...] += dot(x, w_ref[0, :width])
    up[...] += dot(x, w_ref[0, width : 2 * width])
    back[...] += dot(cot_ref[0], w_ref[0, 2 * width :])

    @pl.when(step == pl.num_programs(0) - 1)
    def _():
        gate_pre, up_pre, hidden_grad = gate[...], up[...], back[...]
        sigma = 1.0 / (1.0 + jnp.exp(-gate_pre))
        silu = gate_pre * sigma
        hidden_ref[...] = (silu * up_pre).astype(bf16)
        gate_grad_ref[...] = (
            hidden_grad * up_pre * sigma * (1.0 + gate_pre * (1.0 - sigma))
        ).astype(bf16)
        up_grad_ref[...] = (hidden_grad * silu).astype(bf16)


def cut(total, own_ref, sends):
    rows = own_ref.shape[1]
    own_ref[0] = total[:rows]
    for j, ref in enumerate(sends):
        ref[0] = total[(j + 1) * rows : (j + 2) * rows].astype(bf16)


def two_grad_kernel(gate_grad_ref, up_grad_ref, w_ref, own_ref, *sends):
    width = own_ref.shape[2]
    total = dot(gate_grad_ref[...], w_ref[0, :width], NT) + dot(
        up_grad_ref[...], w_ref[0, width : 2 * width], NT
    )
    cut(total, own_ref, sends)


def down_kernel(hidden_ref, w_ref, own_ref, *sends):
    cut(dot(hidden_ref[...], w_ref[0], NT), own_ref, sends)


def ffn_weights_kernel(peers, *refs):
    blocks = refs[:peers]
    cot_ref, hidden_ref, gate_grad_ref, up_grad_ref, out_ref = refs[peers:]
    width = cot_ref.shape[2]
    x = stacked(blocks)
    out_ref[0, :width] = dot(x, gate_grad_ref[...], TN).astype(bf16)
    out_ref[0, width : 2 * width] = dot(x, up_grad_ref[...], TN).astype(bf16)
    out_ref[0, 2 * width :] = dot(cot_ref[0], hidden_ref[...], TN).astype(bf16)


def norm_back(normal, inv, grad, gain):
    scaled = grad * gain
    inner = row_mean(scaled * normal)
    return inv[None] * (scaled - row_mean(scaled)[None] - normal * inner[None])


def token_sum(x3):
    return jnp.sum(x3, axis=1, keepdims=True)


def mid_back_kernel(mid_ref, cot_ref, gain_ref, own_ref, *refs):
    grad_ref, low_ref, gain_grad_ref, bias_grad_ref = refs[-4:]
    total = own_ref[...]
    for ref in refs[:-4]:
        total = total + ref[...].astype(f32)
    normal, inv = row_stats(mid_ref[...])
    gain_grad_ref[...] = token_sum(total * normal)
    bias_grad_ref[...] = token_sum(total)
    grad = cot_ref[...].astype(f32) + norm_back(normal, inv, total, gain_ref[...])
    grad_ref[...] = grad
    low_ref[...] = grad.astype(bf16)


def block_out_kernel(mid_ref, own_ref, *refs):
    total = mid_ref[...] + own_ref[...]
    for ref in refs[:-1]:
        total = total + ref[...].astype(f32)
    refs[-1][...] = total.astype(bf16)


def attend_back_kernel(
    count, peers, order_ref, at_ref, hide_ref, table_ref, q_ref, here_ref, early_ref, log_ref, *refs
):
    lows = refs[:peers]
    weights = refs[peers : peers + 2 * count]
    low_ref, dq_ref, dhere_ref, dearly_ref, datt = refs[peers + 2 * count :]
    rows, feat = q_ref.shape
    part = rows // peers
    scale = HD**-0.5
    for j in range(peers):
        low_ref[:, pl.ds(pl.multiple_of(at_ref[j] * part, part), part), :] = lows[j][...]
    half = feat // 2
    for h in range(2):
        total = dot(low_ref[order_ref[0]], weights[h * count][...], NT)
        for k in range(1, count):
            total = total + dot(low_ref[order_ref[k]], weights[h * count + k][...], NT)
        datt[:, h * half : (h + 1) * half] = total.astype(bf16)
    for pair in range(feat // (2 * HD)):
        cols = slice(pair * 2 * HD, (pair + 1) * 2 * HD)
        q = q_ref[:, cols]
        k = jnp.concatenate([early_ref[0, :, cols], here_ref[0, :, cols]], axis=0)
        v = jnp.concatenate([early_ref[1, :, cols], here_ref[1, :, cols]], axis=0)
        da = datt[:, cols]
        grads = []
        for h in range(2):
            mask = head_mask(rows, h)
            scores = dot(jnp.where(mask, q, 0), k, NT) * scale + hide_ref[...]
            probs = jnp.exp(scores - log_ref[2 * pair + h])
            weight_grad = dot(jnp.where(mask, da, 0), v, NT)
            inner = jnp.sum(probs * weight_grad, axis=-1, keepdims=True)
            score_grad = (probs * (weight_grad - inner)).astype(bf16)
            grads.append(
                (
                    dot(score_grad, k) * scale,
                    dot(score_grad, q, TN) * scale,
                    dot(probs.astype(bf16), da, TN),
                )
            )
        dq = jnp.where(head_mask(rows, 0), grads[0][0], grads[1][0])
        dq_ref[:, cols] = spin(dq, table_ref[...], -1).astype(bf16)
        for i in (1, 2):
            both = jnp.where(head_mask(2 * rows, 0), grads[0][i], grads[1][i])
            dearly_ref[i - 1, :, cols] = both[:rows].astype(bf16)
            dhere_ref[i - 1, :, cols] = both[rows:]


def out_weights_kernel(count, order_ref, att_ref, low_ref, *outs):
    half = att_ref.shape[1] // 2
    for h in range(2):
        for k in range(count):
            outs[h * count + k][...] = dot(
                att_ref[:, h * half : (h + 1) * half], low_ref[order_ref[k]], TN
            ).astype(bf16)


def one_grad_kernel(
    count, order_ref, at_ref, x_ref, table_ref, dq_ref, dhere_ref, dback_ref, *refs
):
    weights = refs[: 2 * count]
    back_ref, bias_ref, gain_grad_ref, norm_bias_ref, own_ref = refs[2 * count : 2 * count + 5]
    sends = refs[2 * count + 5 : -1]
    part_ref = refs[-1]
    back_ref[0] = dq_ref[...]
    dk = dhere_ref[0] + dback_ref[0].astype(f32)
    back_ref[1] = spin(dk, table_ref[...], -1).astype(bf16)
    back_ref[2] = (dhere_ref[1] + dback_ref[1].astype(f32)).astype(bf16)
    bias_ref[...] = jnp.sum(back_ref[...].astype(f32), axis=1, keepdims=True)
    half = dq_ref.shape[1] // 2
    for k in range(count):
        total = None
        for h in range(2):
            for j in range(3):
                term = dot(
                    back_ref[j, :, h * half : (h + 1) * half], weights[h * count + k][j], NT
                )
                total = term if total is None else total + term
        part_ref[order_ref[k]] = total
    normal, _ = row_stats(split(x_ref[...].astype(f32), count))
    gain_grad_ref[...] = token_sum(part_ref[...] * normal)
    norm_bias_ref[...] = token_sum(part_ref[...])
    hand_out(at_ref, part_ref, own_ref, sends)


def qkv_weights_kernel(count, order_ref, normed_ref, back_ref, *outs):
    half = back_ref.shape[2] // 2
    for h in range(2):
        for k in range(count):
            for j in range(3):
                outs[h * count + k][j] = dot(
                    normed_ref[order_ref[k]], back_ref[j, :, h * half : (h + 1) * half], TN
                ).astype(bf16)


def input_grad_kernel(at_ref, x_ref, gain_ref, mid_grad_ref, own_ref, *refs):
    rows = own_ref.shape[1]
    total = own_ref[...]
    for ref in refs[:-1]:
        total = total + ref[...].astype(f32)
    block = x_ref[pl.ds(pl.multiple_of(at_ref[0] * rows, rows), rows), :].astype(f32)
    normal, inv = row_stats(split(block, own_ref.shape[0]))
    refs[-1][...] = (mid_grad_ref[...] + norm_back(normal, inv, total, gain_ref[...])).astype(bf16)


def join_kernel(at_ref, *refs):
    out_ref = refs[-1]
    slices, rows, width = refs[0].shape
    for j, ref in enumerate(refs[:-1]):
        at = pl.ds(pl.multiple_of(at_ref[j] * rows, rows), rows)
        for n in range(slices):
            out_ref[at, n * width : (n + 1) * width] = ref[n]


def on_device(
    block_in,
    seq_lengths,
    attn_gain,
    attn_bias,
    qkv_weight,
    qkv_bias,
    out_weight,
    ffn_gain,
    ffn_bias,
    gate_up_weight,
    down_weight,
    out_cotangent,
):
    tok, model = block_in.shape
    feat = qkv_weight.shape[2]
    hid = down_weight.shape[0]
    plane = Plane()
    count = plane.count
    width = model // count
    peers = lax.axis_size("tensor")
    chunk = tok // peers
    heads = feat // HD
    order = plane.me ^ jnp.arange(count, dtype=jnp.int32)
    at = lax.axis_index("tensor") ^ jnp.arange(peers, dtype=jnp.int32)

    half = feat // 2
    qkv_slots = plane.gather((qkv_weight[:, :, :half], qkv_weight[:, :, half:]))
    out_slots = plane.gather((out_weight[:half], out_weight[half:]))
    qkv_list = [qkv_slots[h][k] for h in range(2) for k in range(count)]
    out_list = [out_slots[h][k] for h in range(2) for k in range(count)]
    ffn_shard = jnp.concatenate([gate_up_weight[0], gate_up_weight[1], down_weight.T], axis=0)
    ffn_all = lax.all_gather(ffn_shard, PLANE, axis=0, tiled=False)

    offset = lax.axis_index("context") * tok
    places = offset + jnp.arange(tok, dtype=jnp.int32)
    lengths = seq_lengths[0]
    ends = jnp.cumsum(lengths)
    starts = jnp.sum(jnp.where(ends[None, :] <= places[:, None], lengths[None, :], 0), axis=1)
    turn = ROT // 2
    frequency = jnp.exp(jnp.arange(turn).astype(f32) * (-2.0 * math.log(10000.0) / ROT))
    angles = (places - starts).astype(f32)[:, None] * frequency[None, :]
    cosine = jnp.tile(jnp.cos(angles), (1, 128 // turn))
    sine = jnp.tile(jnp.sin(angles), (1, 128 // turn))
    lane = jnp.arange(128)[None, :] % HD
    tables = jnp.stack(
        [
            jnp.where(lane < ROT, cosine, 1.0),
            jnp.where(lane < turn, -sine, 0.0),
            jnp.where((lane >= turn) & (lane < ROT), sine, 0.0),
        ]
    )
    key_places = offset - tok + jnp.arange(2 * tok, dtype=jnp.int32)
    visible = (key_places[None, :] <= places[:, None]) & (key_places[None, :] >= starts[:, None])
    hide = jnp.where(visible, 0.0, NEG).astype(f32)

    by_slice = lambda vec: vec.reshape(count, 1, width)
    normed_one = call(
        norm_kernel, "norm_one", shape((count, tok, width), bf16),
        (block_in, by_slice(attn_gain), by_slice(attn_bias)), [VM] * 3,
    )
    cot = call(
        reorder_kernel, "cotangent_rows", shape((count, tok, width), bf16),
        (at, out_cotangent), [SM, VM],
    )

    queries, here = call(
        functools.partial(qkv_kernel, count), "qkv",
        (shape((tok, feat), bf16), shape((2, tok, feat), bf16)),
        (order, normed_one, qkv_bias.reshape(3, 1, feat), tables, *qkv_list),
        [SM] + [VM] * (3 + 2 * count), flops=6 * tok * model * feat, moved=6 * model * feat,
    )
    early = lax.ppermute(here, "context", [(i, i + 1) for i in range(plane.context - 1)])
    sends = [shape((count, chunk, width), bf16)] * (peers - 1)
    own_shape = shape((count, chunk, width), f32)
    attended, logs, own, *parts = call(
        functools.partial(attend_kernel, count), "attend",
        (shape((tok, feat), bf16), shape((heads, tok, 1), f32), own_shape, *sends),
        (order, at, hide, queries, here, early, *out_list),
        [SM, SM] + [VM] * (4 + 2 * count),
        scratch=[pltpu.VMEM((count, tok, width), f32)],
        flops=8 * tok * tok * feat + 2 * tok * model * feat, moved=2 * model * feat,
    )
    got = tensor_exchange([None] + parts)
    mid, normed_chunk = call(
        mid_kernel, "mid", (own_shape, sends[0]),
        (at, block_in, by_slice(ffn_gain), by_slice(ffn_bias), own, *got),
        [SM] + [VM] * (4 + len(got)),
    )
    normed_two = tensor_gather(normed_chunk)

    big = pltpu.CompilerParams(vmem_limit_bytes=56 * 2**20, dimension_semantics=("arbitrary",))
    by_n = lambda *dims: pl.BlockSpec((1,) + dims, lambda n: (n,) + (0,) * len(dims))
    whole = lambda *dims: pl.BlockSpec(dims, lambda n: (0,) * len(dims))
    hid_shape = shape((tok, hid), bf16)
    hidden, gate_grad, up_grad = pl.pallas_call(
        functools.partial(ffn_kernel, peers),
        name="ffn",
        grid=(count,),
        out_shape=(hid_shape,) * 3,
        in_specs=[by_n(chunk, width)] * peers + [by_n(tok, width), by_n(3 * width, hid)],
        out_specs=[whole(tok, hid)] * 3,
        scratch_shapes=[pltpu.VMEM((tok, hid), f32)] * 3,
        compiler_params=big,
        cost_estimate=pl.CostEstimate(
            flops=6 * tok * model * hid, bytes_accessed=6 * model * hid, transcendentals=0
        ),
    )(*normed_two, cot, ffn_all)
    grad_own, *grad_parts = pl.pallas_call(
        two_grad_kernel,
        name="two_grad",
        grid=(count,),
        out_shape=(own_shape, *sends),
        in_specs=[whole(tok, hid)] * 2 + [by_n(2 * width, hid)],
        out_specs=[by_n(chunk, width)] * peers,
        compiler_params=big,
        cost_estimate=pl.CostEstimate(
            flops=4 * tok * model * hid, bytes_accessed=4 * model * hid, transcendentals=0
        ),
    )(gate_grad, up_grad, ffn_all)
    got = tensor_exchange([None] + grad_parts)
    ffn_grads = pl.pallas_call(
        functools.partial(ffn_weights_kernel, peers),
        name="ffn_weights",
        grid=(count,),
        out_shape=shape((count, 3 * width, hid), bf16),
        in_specs=[by_n(chunk, width)] * peers + [by_n(tok, width)] + [whole(tok, hid)] * 3,
        out_specs=by_n(3 * width, hid),
        compiler_params=big,
        cost_estimate=pl.CostEstimate(
            flops=6 * tok * model * hid, bytes_accessed=6 * model * hid, transcendentals=0
        ),
    )(*normed_two, cot, hidden, gate_grad, up_grad)
    ffn_total = lax.psum_scatter(ffn_grads, PLANE, scatter_dimension=0, tiled=False)
    down_own, *down_parts = pl.pallas_call(
        down_kernel,
        name="down",
        grid=(count,),
        out_shape=(own_shape, *sends),
        in_specs=[whole(tok, hid), pl.BlockSpec((1, width, hid), lambda n: (n, 2, 0))],
        out_specs=[by_n(chunk, width)] * peers,
        compiler_params=big,
        cost_estimate=pl.CostEstimate(
            flops=2 * tok * model * hid, bytes_accessed=2 * model * hid, transcendentals=0
        ),
    )(hidden, ffn_all)
    vec = shape((count, 1, width), f32)
    mid_grad, low_chunk, ffn_gain_grad, ffn_bias_grad = call(
        mid_back_kernel, "mid_back", (own_shape, sends[0], vec, vec),
        (mid, cot[:, :chunk], by_slice(ffn_gain), grad_own, *got),
        [VM] * (4 + len(got)),
    )
    low_blocks = tensor_gather(low_chunk)
    down_got = tensor_exchange([None] + down_parts)
    out_chunk = call(
        block_out_kernel, "block_out", sends[0], (mid, down_own, *down_got),
        [VM] * (2 + len(down_got)),
    )
    block_out = call(
        join_kernel, "block_out_rows", shape((tok, model), bf16),
        (at, *tensor_gather(out_chunk)), [SM] + [VM] * peers,
    )

    low, dq, dhere, dearly = call(
        functools.partial(attend_back_kernel, count, peers), "attend_back",
        (
            shape((count, tok, width), bf16), shape((tok, feat), bf16),
            shape((2, tok, feat), f32), shape((2, tok, feat), bf16),
        ),
        (order, at, hide, tables, queries, here, early, logs, *low_blocks, *out_list),
        [SM, SM] + [VM] * (6 + peers + 2 * count),
        scratch=[pltpu.VMEM((tok, feat), bf16)],
        flops=20 * tok * tok * feat + 2 * tok * model * feat, moved=2 * model * feat,
    )
    dback = lax.ppermute(dearly, "context", [(i + 1, i) for i in range(plane.context - 1)])
    out_grads = call(
        functools.partial(out_weights_kernel, count), "out_weights",
        (shape((half, width), bf16),) * (2 * count),
        (order, attended, low), [SM, VM, VM],
        flops=2 * tok * model * feat, moved=2 * model * feat,
    )
    out_a, out_b = plane.scatter(
        [{k: out_grads[h * count + k] for k in range(count)} for h in range(2)]
    )
    back, bias_grad, attn_gain_grad, attn_bias_grad, own, *parts = call(
        functools.partial(one_grad_kernel, count), "one_grad",
        (
            shape((3, tok, feat), bf16), shape((3, 1, feat), f32), vec, vec, own_shape, *sends,
        ),
        (order, at, block_in, tables, dq, dhere, dback, *qkv_list),
        [SM, SM] + [VM] * (5 + 2 * count),
        scratch=[pltpu.VMEM((count, tok, width), f32)],
        flops=6 * tok * model * feat, moved=6 * model * feat,
    )
    got = tensor_exchange([None] + parts)
    qkv_grads = call(
        functools.partial(qkv_weights_kernel, count), "qkv_weights",
        (shape((3, width, half), bf16),) * (2 * count),
        (order, normed_one, back), [SM, VM, VM],
        flops=6 * tok * model * feat, moved=6 * model * feat,
    )
    qkv_a, qkv_b = plane.scatter(
        [{k: qkv_grads[h * count + k] for k in range(count)} for h in range(2)]
    )
    grad_chunk = call(
        input_grad_kernel, "input_grad", sends[0],
        (at, block_in, by_slice(attn_gain), mid_grad, own, *got),
        [SM] + [VM] * (4 + len(got)),
    )
    input_grad = call(
        join_kernel, "input_grad_rows", shape((tok, model), bf16),
        (at, *tensor_gather(grad_chunk)), [SM] + [VM] * peers,
    )

    vectors = jnp.stack(
        [v.reshape(model) for v in (attn_gain_grad, attn_bias_grad, ffn_gain_grad, ffn_bias_grad)]
    )
    vectors = plane.total(vectors, True)
    qkv_bias_grad = plane.total(bias_grad.reshape(3, feat), False)

    return (
        block_out,
        input_grad,
        vectors[0],
        vectors[1],
        jnp.concatenate([qkv_a, qkv_b], axis=2),
        qkv_bias_grad,
        jnp.concatenate([out_a, out_b], axis=0),
        vectors[2],
        vectors[3],
        ffn_total[: 2 * width].reshape(2, width, hid).astype(f32),
        ffn_total[2 * width :].T.astype(f32),
    )


def solution(mesh):
    in_specs = (
        P(("fsdp", "context"), None),
        P("fsdp", None),
        P(),
        P(),
        P(None, ("fsdp", "context"), "tensor"),
        P(None, "tensor"),
        P("tensor", ("fsdp", "context")),
        P(),
        P(),
        P(None, ("fsdp", "context"), "tensor"),
        P("tensor", ("fsdp", "context")),
        P(("fsdp", "context"), None),
    )
    out_specs = (
        P(("fsdp", "context"), None),
        P(("fsdp", "context"), None),
        P(),
        P(),
        P(None, ("fsdp", "context"), "tensor"),
        P(None, "tensor"),
        P("tensor", ("fsdp", "context")),
        P(),
        P(),
        P(None, ("fsdp", "context"), "tensor"),
        P("tensor", ("fsdp", "context")),
    )
    return jax.shard_map(
        on_device, mesh=mesh, in_specs=in_specs, out_specs=out_specs, check_vma=False
    )
```

```python
import functools
import math

import jax
import jax.numpy as jnp
from jax import lax
from jax.experimental import pallas as pl
from jax.experimental.pallas import tpu as pltpu
from jax.sharding import PartitionSpec as P

HD = 64
ROT = 16
EPS = 1e-05
NEG = -1e30
f32 = jnp.float32
bf16 = jnp.bfloat16
VM = pl.BlockSpec(memory_space=pltpu.VMEM)
SM = pl.BlockSpec(memory_space=pltpu.SMEM)
HB = pl.BlockSpec(memory_space=pl.ANY)
PLANE = ("fsdp", "context")


def shape(dims, dtype):
    return jax.ShapeDtypeStruct(tuple(dims), dtype)


WEIGHT = dict(qkv=10, mid=20, mid_back=60, attend_back=200, input_grad=20, input_grad_rows=20)


def params(name):
    return dict(
        name=name,
        compiler_params=pltpu.CompilerParams(vmem_limit_bytes=56 * 2**20),
        cost_estimate=pl.CostEstimate(
            flops=int(1.15e9 * WEIGHT.get(name, 0)), bytes_accessed=0, transcendentals=0
        ),
    )


def call(kernel, name, outs, args, specs, scratch=()):
    return pl.pallas_call(
        kernel,
        out_shape=outs,
        in_specs=specs,
        out_specs=jax.tree.map(lambda _: VM, outs),
        scratch_shapes=list(scratch),
        **params(name),
    )(*args)


def dot(a, b, dims=((1,), (0,))):
    return lax.dot_general(a, b, (dims, ((), ())), preferred_element_type=f32)


NT = ((1,), (1,))
TN = ((0,), (0,))


def tie(value, *others):
    return lax.optimization_barrier((value, others))[0]


class Plane:
    def __init__(self):
        self.fsdp = lax.axis_size("fsdp")
        self.context = lax.axis_size("context")
        self.count = self.fsdp * self.context
        self.me = lax.axis_index("fsdp") * self.context + lax.axis_index("context")
        self.core = self.context
        bits = [1 << i for i in range(int(math.log2(self.count))) if (1 << i) != self.core]
        self.up, self.down = bits, bits[::-1]
        self.kept = [k for k in range(self.count) if not k & self.core]
        self.sent = [k ^ self.core for k in self.kept]
        own = [[d for d in range(self.count) if d & self.core == c] for c in (0, self.core)]
        self.groups = own

    def rank(self, k):
        low = self.core - 1
        squeeze = lambda d: (d & low) | ((d >> 1) & ~low)
        return squeeze(self.me) ^ squeeze(k)

    def swap(self, value, bit):
        if bit < self.context:
            pairs = [(i, i ^ bit) for i in range(self.context)]
            return lax.ppermute(value, "context", pairs)
        step = bit // self.context
        pairs = [(i, i ^ step) for i in range(self.fsdp)]
        return lax.ppermute(value, "fsdp", pairs)

    def across(self, value):
        return jax.tree.map(lambda v: self.swap(v, self.core), value)

    def gather(self, shard, order, *after):
        slots = {0: shard}
        for bit in order + [self.core]:
            for k in list(slots):
                wait = after if k and bit != self.core else ()
                slots[k ^ bit] = self.swap(tie(slots[k], wait) if wait else slots[k], bit)
        return slots

    def gather_halves(self, shard, *prepared):
        if len(self.up) != 2:
            return {k: (v,) for k, v in self.gather(shard, self.up).items()}
        y, x = self.up
        half = shard.shape[-1] // 2
        over_x, over_y = self.swap(shard, x), self.swap(shard, y)
        first, second = tie((over_x[..., :half], over_y[..., half:]), prepared)
        both = (self.swap(first, y), self.swap(second, x))
        slots = {0: (shard,), x: (over_x,), y: (over_y,), x ^ y: both}
        return slots | {k ^ self.core: self.across(v) for k, v in slots.items()}

    def halves(self, order):
        slots = sorted(self.kept, key=lambda k: tuple(not k & bit for bit in order))
        return slots[: len(slots) // 2], slots[len(slots) // 2 :]

    def total(self, value):
        bit = 1
        while bit < self.count:
            value = value + self.swap(value, bit)
            bit *= 2
        return value


class Scatter:
    def __init__(self, plane, first, second, order):
        self.plane, self.order = plane, list(order)
        self.low, self.terms = first, [second]

    def step(self, *after):
        got = self.plane.swap(tie(self.low, after), self.order.pop(0))
        self.terms.append(got)
        if self.order:
            rest = got.shape[0] // 2
            self.low = sum(t[:rest].astype(f32) for t in self.terms).astype(bf16)
            self.terms = [t[rest:] for t in self.terms]
        return got

    def total(self, *after):
        while self.order:
            self.step(*after)
        return sum(t[0].astype(f32) for t in self.terms)


def tensor_swap(value, j):
    peers = lax.axis_size("tensor")
    return lax.ppermute(value, "tensor", [(i, i ^ j) for i in range(peers)])


def tensor_exchange(parts):
    return [tensor_swap(part, j) for j, part in enumerate(parts) if j]


def tensor_gather(part):
    return [part] + [tensor_swap(part, j) for j in range(1, lax.axis_size("tensor"))]


def row_stats(x3):
    size = x3.shape[0] * x3.shape[2]
    mean = jnp.sum(jnp.sum(x3, axis=0), axis=-1, keepdims=True) / size
    center = x3 - mean[None]
    var = jnp.sum(jnp.sum(center * center, axis=0), axis=-1, keepdims=True) / size
    inv = lax.rsqrt(var + EPS)
    return center * inv[None], inv


def row_mean(x3):
    return jnp.sum(jnp.sum(x3, axis=0), axis=-1, keepdims=True) / (x3.shape[0] * x3.shape[2])


def split(x, count):
    width = x.shape[1] // count
    return jnp.stack([x[:, i * width : (i + 1) * width] for i in range(count)])


def by_slot(slots, order_ref, from_ref, kept_ref, sent_ref):
    for ref, which in zip((kept_ref, sent_ref), slots):
        for i, k in enumerate(which):
            ref[i] = from_ref[order_ref[k]]


def norm_kernel(slots, order_ref, x_ref, gain_ref, bias_ref, kept_ref, sent_ref, normed):
    normal, _ = row_stats(split(x_ref[...].astype(f32), normed.shape[0]))
    normed[...] = (normal * gain_ref[...] + bias_ref[...]).astype(bf16)
    by_slot(slots, order_ref, normed, kept_ref, sent_ref)


def reorder_kernel(slots, order_ref, at_ref, x_ref, out_ref, kept_ref, sent_ref, slices):
    rows = x_ref.shape[0] // at_ref.shape[0]
    for j in range(at_ref.shape[0]):
        block = x_ref[pl.ds(pl.multiple_of(at_ref[j] * rows, rows), rows), :]
        out_ref[j * rows : (j + 1) * rows, :] = block
        slices[:, j * rows : (j + 1) * rows, :] = split(block, slices.shape[0])
    by_slot(slots, order_ref, slices, kept_ref, sent_ref)


def spin(x, tables, sign):
    parts = []
    for i in range(x.shape[1] // 128):
        v = x[:, i * 128 : (i + 1) * 128]
        turned = pltpu.roll(v, 128 - ROT // 2, 1) * tables[1] + pltpu.roll(v, ROT // 2, 1) * tables[2]
        parts.append(v * tables[0] + (turned if sign > 0 else -turned))
    return jnp.concatenate(parts, axis=1)


def take(refs, lengths):
    groups, at = [], 0
    for n in lengths:
        groups.append(refs[at : at + n])
        at += n
    return groups, refs[at:]


def qkv_kernel(slots, pieces, kept_ref, sent_ref, bias_ref, table_ref, *refs):
    weights, (q_ref, kv_ref) = take(refs, pieces)
    feat = q_ref.shape[1]
    x = {k: ref[i] for ref, which in zip((kept_ref, sent_ref), slots) for i, k in enumerate(which)}
    for cols in tiles(feat):
        for j in range(3):
            total = bias_ref[j, :, cols]
            for k, parts in enumerate(weights):
                part, at = parts[cols.start * len(parts) // feat], cols.start % (feat // len(parts))
                total = total + dot(x[k], part[j, :, at : at + cols.stop - cols.start])
            if j < 2:
                total = spin(total, table_ref[...], 1)
            if j == 0:
                q_ref[:, cols] = total.astype(bf16)
            else:
                kv_ref[j - 1, :, cols] = total.astype(bf16)


def head_mask(rows, h):
    lane = lax.broadcasted_iota(jnp.int32, (rows, 2 * HD), 1)
    return (lane // HD) == h


def attend_kernel(count, order_ref, at_ref, hide_ref, q_ref, here_ref, early_ref, *refs):
    weights = refs[:count]
    att_ref, log_ref, own_ref = refs[count : count + 3]
    sends = refs[count + 3 : -1]
    part_ref = refs[-1]
    rows, feat = q_ref.shape
    scale = HD**-0.5
    for pair in range(feat // (2 * HD)):
        cols = slice(pair * 2 * HD, (pair + 1) * 2 * HD)
        q = q_ref[:, cols]
        k = jnp.concatenate([early_ref[0, :, cols], here_ref[0, :, cols]], axis=0)
        v = jnp.concatenate([early_ref[1, :, cols], here_ref[1, :, cols]], axis=0)
        out = []
        for h in range(2):
            mask = head_mask(rows, h)
            scores = dot(jnp.where(mask, q, 0), k, NT) * scale + hide_ref[...]
            top = jnp.max(scores, axis=-1, keepdims=True)
            exps = jnp.exp(scores - top)
            total = jnp.sum(exps, axis=-1, keepdims=True)
            log_ref[2 * pair + h] = top + jnp.log(total)
            out.append(dot((exps / total).astype(bf16), v))
        att_ref[:, cols] = jnp.where(head_mask(rows, 0), out[0], out[1]).astype(bf16)
    for k in range(count):
        part_ref[order_ref[k]] = dot(att_ref[...], weights[k][...])
    hand_out(at_ref, part_ref, own_ref, sends)


def hand_out(at_ref, part_ref, own_ref, sends):
    rows = own_ref.shape[1]
    for j in range(at_ref.shape[0]):
        block = part_ref[:, pl.ds(pl.multiple_of(at_ref[j] * rows, rows), rows), :]
        if j == 0:
            own_ref[...] = block
        else:
            sends[j - 1][...] = block.astype(bf16)


def ffn_out_kernel(total_ref, gate_up_ref, down_ref):
    width = down_ref.shape[1]
    for i in range(2):
        gate_up_ref[i] = total_ref[i * width : (i + 1) * width].astype(f32)
    down_ref[...] = total_ref[2 * width :].astype(f32).T


def mid_kernel(at_ref, x_ref, gain_ref, bias_ref, own_ref, *refs):
    mid_ref, normed_ref = refs[-2:]
    rows = own_ref.shape[1]
    total = own_ref[...]
    for ref in refs[:-2]:
        total = total + ref[...].astype(f32)
    block = x_ref[pl.ds(pl.multiple_of(at_ref[0] * rows, rows), rows), :].astype(f32)
    mid = split(block, own_ref.shape[0]) + total
    mid_ref[...] = mid
    normal, _ = row_stats(mid)
    normed_ref[...] = (normal * gain_ref[...] + bias_ref[...]).astype(bf16)


def pack_kernel(gate_up_ref, down_ref, out_ref):
    width = down_ref.shape[1]
    out_ref[:width] = gate_up_ref[0]
    out_ref[width : 2 * width] = gate_up_ref[1]
    out_ref[2 * width :] = down_ref[...].T


def fetch(all_ref, which, to_ref, sem):
    count, rows, _ = all_ref.shape
    width = rows // 3
    copies = [
        pltpu.make_async_copy(
            all_ref.at[n, pl.ds(which * width, width)], to_ref.at[pl.ds(n * width, width)], sem.at[n]
        )
        for n in range(count)
    ]
    for copy in copies:
        copy.start()
    return copies


def tiles(size, step=256):
    return [slice(i, min(i + step, size)) for i in range(0, size, step)]


def ffn_kernel(slots, peers, order_ref, *refs):
    blocks = refs[:peers]
    cot_ref, all_ref, kept_ref, sent_ref, hidden_ref, gate_grad_ref, up_grad_ref, own_ref = refs[
        peers : peers + 8
    ]
    sends, (gate, up, down, sems, x_ref, pre_ref) = refs[peers + 8 : -6], refs[-6:]
    copies = [fetch(all_ref, i, ref, sems.at[i]) for i, ref in enumerate((gate, up, down))]
    rows, width = own_ref.shape[1:]
    for j, ref in enumerate(blocks):
        at = slice(j * rows, (j + 1) * rows)
        for n in range(own_ref.shape[0]):
            x_ref[at, n * width : (n + 1) * width] = ref[n]
        for to_ref, which in zip((kept_ref, sent_ref), slots):
            for i, k in enumerate(which):
                to_ref[i, at, :] = ref[order_ref[k]]
    x = x_ref[...]
    for copy in copies[0]:
        copy.wait()
    for cols in tiles(hidden_ref.shape[1]):
        pre_ref[:, cols] = dot(x, gate[:, cols])
    for copy in copies[1] + copies[2]:
        copy.wait()
    for cols in tiles(hidden_ref.shape[1]):
        gate_pre = pre_ref[:, cols]
        up_pre = dot(x, up[:, cols])
        hidden_grad = dot(cot_ref[...], down[:, cols])
        sigma = 1.0 / (1.0 + jnp.exp(-gate_pre))
        silu = gate_pre * sigma
        hidden_ref[:, cols] = (silu * up_pre).astype(bf16)
        gate_grad_ref[:, cols] = (
            hidden_grad * up_pre * sigma * (1.0 + gate_pre * (1.0 - sigma))
        ).astype(bf16)
        up_grad_ref[:, cols] = (hidden_grad * silu).astype(bf16)
    for n in range(own_ref.shape[0]):
        at = slice(n * width, (n + 1) * width)
        total = dot(gate_grad_ref[...], gate[at], NT) + dot(up_grad_ref[...], up[at], NT)
        cut(n, total, own_ref, sends)


def cut(n, total, own_ref, sends):
    rows = own_ref.shape[1]
    own_ref[n] = total[:rows]
    for j, ref in enumerate(sends):
        ref[n] = total[(j + 1) * rows : (j + 2) * rows].astype(bf16)


def down_kernel(at_ref, hidden_ref, all_ref, mid_ref, out_ref, down, sem):
    for copy in fetch(all_ref, 2, down, sem):
        copy.wait()
    count, rows, width = mid_ref.shape
    for n in range(count):
        at = slice(n * width, (n + 1) * width)
        total = dot(hidden_ref[...], down[at], NT)
        for j in range(at_ref.shape[0]):
            block = total[j * rows : (j + 1) * rows]
            block = block + mid_ref[n] if j == 0 else block
            out_ref[pl.ds(pl.multiple_of(at_ref[j] * rows, rows), rows), at] = block.astype(bf16)


def ffn_weights_kernel(place_ref, *refs):
    x, cot, grads, out_ref = refs[:2], refs[2:4], refs[4:10], refs[10]
    width = x[0].shape[2]
    for i, left in enumerate((x, x, cot)):
        total = dot(left[0][0], grads[2 * i][...], TN) + dot(left[1][0], grads[2 * i + 1][...], TN)
        out_ref[i * width : (i + 1) * width] = total.astype(bf16)


def norm_back(normal, inv, grad, gain):
    scaled = grad * gain
    inner = row_mean(scaled * normal)
    return inv[None] * (scaled - row_mean(scaled)[None] - normal * inner[None])


def token_sum(x3):
    return jnp.sum(x3, axis=1, keepdims=True)


def mid_back_kernel(mid_ref, cot_ref, gain_ref, own_ref, *refs):
    grad_ref, low_ref, gain_grad_ref, bias_grad_ref = refs[-4:]
    total = own_ref[...]
    for ref in refs[:-4]:
        total = total + ref[...].astype(f32)
    normal, inv = row_stats(mid_ref[...])
    gain_grad_ref[...] = token_sum(total * normal)
    bias_grad_ref[...] = token_sum(total)
    cot = split(cot_ref[: mid_ref.shape[1]].astype(f32), mid_ref.shape[0])
    grad = cot + norm_back(normal, inv, total, gain_ref[...])
    grad_ref[...] = grad
    low_ref[...] = grad.astype(bf16)


def attend_back_kernel(
    slots, peers, order_ref, at_ref, hide_ref, table_ref, q_ref, here_ref, early_ref, log_ref, *refs
):
    count = order_ref.shape[0]
    lows = refs[:peers]
    weights = refs[peers : peers + count]
    kept_ref, sent_ref, dq_ref, dhere_ref, dearly_ref, datt = refs[peers + count :]
    rows, feat = q_ref.shape
    part = rows // peers
    scale = HD**-0.5
    low = {}
    for ref, which in zip((kept_ref, sent_ref), slots):
        for i, k in enumerate(which):
            low[k] = ref.at[i]
            for j in range(peers):
                at = pl.ds(pl.multiple_of(at_ref[j] * part, part), part)
                ref[i, at, :] = lows[j][order_ref[k]]
    for cols in tiles(feat):
        total = dot(low[0][...], weights[0][cols], NT)
        for k in range(1, count):
            total = total + dot(low[k][...], weights[k][cols], NT)
        datt[:, cols] = total.astype(bf16)
    for pair in range(feat // (2 * HD)):
        cols = slice(pair * 2 * HD, (pair + 1) * 2 * HD)
        q = q_ref[:, cols]
        k = jnp.concatenate([early_ref[0, :, cols], here_ref[0, :, cols]], axis=0)
        v = jnp.concatenate([early_ref[1, :, cols], here_ref[1, :, cols]], axis=0)
        da = datt[:, cols]
        grads = []
        for h in range(2):
            mask = head_mask(rows, h)
            scores = dot(jnp.where(mask, q, 0), k, NT) * scale + hide_ref[...]
            probs = jnp.exp(scores - log_ref[2 * pair + h])
            weight_grad = dot(jnp.where(mask, da, 0), v, NT)
            inner = jnp.sum(probs * weight_grad, axis=-1, keepdims=True)
            score_grad = (probs * (weight_grad - inner)).astype(bf16)
            grads.append(
                (
                    dot(score_grad, k) * scale,
                    dot(score_grad, q, TN) * scale,
                    dot(probs.astype(bf16), da, TN),
                )
            )
        dq = jnp.where(head_mask(rows, 0), grads[0][0], grads[1][0])
        dq_ref[:, cols] = spin(dq, table_ref[...], -1).astype(bf16)
        for i in (1, 2):
            both = jnp.where(head_mask(2 * rows, 0), grads[0][i], grads[1][i])
            dearly_ref[i - 1, :, cols] = both[:rows].astype(bf16)
            dhere_ref[i - 1, :, cols] = both[rows:]


def out_weights_kernel(slots, halves, *refs):
    att, low, outs = refs[:2], refs[2:4], refs[4:]
    part = att[0].shape[1] // 2
    for h, both in enumerate(halves):
        cols = slice(h * part, (h + 1) * part)
        for ref, which in zip(outs[2 * h :], both):
            for i, k in enumerate(which):
                at = slots[0].index(k)
                total = dot(att[0][:, cols], low[0][at], TN) + dot(att[1][:, cols], low[1][at], TN)
                ref[i] = total.astype(bf16)


def one_grad_kernel(
    pieces, order_ref, at_ref, x_ref, table_ref, dq_ref, dhere_ref, dback_ref, *refs
):
    weights, refs = take(refs, pieces)
    *back_refs, bias_ref, gain_grad_ref, norm_bias_ref, own_ref = refs[:7]
    sends, part_ref = refs[7:-1], refs[-1]
    back_refs[0][...] = dq_ref[...]
    dk = dhere_ref[0] + dback_ref[0].astype(f32)
    back_refs[1][...] = spin(dk, table_ref[...], -1).astype(bf16)
    back_refs[2][...] = (dhere_ref[1] + dback_ref[1].astype(f32)).astype(bf16)
    for j, ref in enumerate(back_refs):
        bias_ref[j] = jnp.sum(ref[...].astype(f32), axis=0, keepdims=True)
    for k, parts in enumerate(weights):
        total, at = None, 0
        for part in parts:
            size = part.shape[2]
            for j, ref in enumerate(back_refs):
                term = dot(ref[:, at : at + size], part[j], NT)
                total = term if total is None else total + term
            at += size
        part_ref[order_ref[k]] = total
    normal, _ = row_stats(split(x_ref[...].astype(f32), len(weights)))
    gain_grad_ref[...] = token_sum(part_ref[...] * normal)
    norm_bias_ref[...] = token_sum(part_ref[...])
    hand_out(at_ref, part_ref, own_ref, sends)


def qkv_weights_kernel(slots, halves, *refs):
    x, grads, outs = refs[:2], refs[2:8], refs[8:]
    part = grads[0].shape[1] // 2
    for h, both in enumerate(halves):
        cols = slice(h * part, (h + 1) * part)
        for ref, which in zip(outs[2 * h :], both):
            for i, k in enumerate(which):
                at = slots[0].index(k)
                for j in range(3):
                    total = dot(x[0][at], grads[j][:, cols], TN)
                    total = total + dot(x[1][at], grads[3 + j][:, cols], TN)
                    ref[i, j] = total.astype(bf16)


def input_grad_kernel(at_ref, x_ref, gain_ref, mid_grad_ref, own_ref, *refs):
    rows = own_ref.shape[1]
    total = own_ref[...]
    for ref in refs[:-1]:
        total = total + ref[...].astype(f32)
    block = x_ref[pl.ds(pl.multiple_of(at_ref[0] * rows, rows), rows), :].astype(f32)
    normal, inv = row_stats(split(block, own_ref.shape[0]))
    refs[-1][...] = (mid_grad_ref[...] + norm_back(normal, inv, total, gain_ref[...])).astype(bf16)


def join_kernel(at_ref, *refs):
    out_ref = refs[-1]
    slices, rows, width = refs[0].shape
    for j, ref in enumerate(refs[:-1]):
        at = pl.ds(pl.multiple_of(at_ref[j] * rows, rows), rows)
        for n in range(slices):
            out_ref[at, n * width : (n + 1) * width] = ref[n]


def on_device(
    block_in,
    seq_lengths,
    attn_gain,
    attn_bias,
    qkv_weight,
    qkv_bias,
    out_weight,
    ffn_gain,
    ffn_bias,
    gate_up_weight,
    down_weight,
    out_cotangent,
):
    tok, model = block_in.shape
    feat = qkv_weight.shape[2]
    hid = down_weight.shape[0]
    plane = Plane()
    count = plane.count
    width = model // count
    peers = lax.axis_size("tensor")
    chunk = tok // peers
    heads = feat // HD
    order = plane.me ^ jnp.arange(count, dtype=jnp.int32)
    at = lax.axis_index("tensor") ^ jnp.arange(peers, dtype=jnp.int32)

    offset = lax.axis_index("context") * tok
    places = offset + jnp.arange(tok, dtype=jnp.int32)
    lengths = seq_lengths[0]
    ends = jnp.cumsum(lengths)
    starts = jnp.sum(jnp.where(ends[None, :] <= places[:, None], lengths[None, :], 0), axis=1)
    turn = ROT // 2
    frequency = jnp.exp(jnp.arange(turn).astype(f32) * (-2.0 * math.log(10000.0) / ROT))
    angles = (places - starts).astype(f32)[:, None] * frequency[None, :]
    cosine = jnp.tile(jnp.cos(angles), (1, 128 // turn))
    sine = jnp.tile(jnp.sin(angles), (1, 128 // turn))
    lane = jnp.arange(128)[None, :] % HD
    tables = jnp.stack(
        [
            jnp.where(lane < ROT, cosine, 1.0),
            jnp.where(lane < turn, -sine, 0.0),
            jnp.where((lane >= turn) & (lane < ROT), sine, 0.0),
        ]
    )
    key_places = offset - tok + jnp.arange(2 * tok, dtype=jnp.int32)
    visible = (key_places[None, :] <= places[:, None]) & (key_places[None, :] >= starts[:, None])
    hide = jnp.where(visible, 0.0, NEG).astype(f32)

    by_slice = lambda vec: vec.reshape(count, 1, width)
    slots = (plane.kept, plane.sent)
    slice_pair = (shape((count // 2, tok, width), bf16),) * 2
    slices = pltpu.VMEM((count, tok, width), bf16)
    one_kept, one_sent = call(
        functools.partial(norm_kernel, slots), "norm_one", slice_pair,
        (order, block_in, by_slice(attn_gain), by_slice(attn_bias)), [SM] + [VM] * 3,
        scratch=[slices],
    )
    cot, cot_kept, cot_sent = call(
        functools.partial(reorder_kernel, slots), "cotangent_rows",
        (shape((tok, model), bf16), *slice_pair), (order, at, out_cotangent), [SM, SM, VM],
        scratch=[slices],
    )

    qkv_slots = plane.gather_halves(qkv_weight, one_kept, one_sent, tables, hide, cot)
    pieces = [len(qkv_slots[k]) for k in range(count)]
    qkv_list = [piece for k in range(count) for piece in qkv_slots[k]]
    first = (qkv_slots[plane.up[0]], qkv_slots[plane.up[-1]])
    passed = qkv_slots[plane.up[0] ^ plane.up[-1]]
    ffn_shard = call(
        pack_kernel, "ffn_shard", shape((3 * width, hid), bf16), (gate_up_weight, down_weight),
        [VM, VM],
    )
    out_slots = plane.gather(tie(out_weight, ffn_shard), plane.up, passed)
    out_list = [out_slots[k] for k in range(count)]
    ffn_all = lax.all_gather(tie(ffn_shard, first), PLANE, axis=0, tiled=False)

    queries, here = call(
        functools.partial(qkv_kernel, slots, pieces), "qkv",
        (shape((tok, feat), bf16), shape((2, tok, feat), bf16)),
        (one_kept, one_sent, qkv_bias.reshape(3, 1, feat), tables, *qkv_list),
        [VM] * (4 + sum(pieces)),
    )
    early = lax.ppermute(here, "context", [(i, i + 1) for i in range(plane.context - 1)])
    sends = [shape((count, chunk, width), bf16)] * (peers - 1)
    own_shape = shape((count, chunk, width), f32)
    attended, logs, own, *parts = call(
        functools.partial(attend_kernel, count), "attend",
        (shape((tok, feat), bf16), shape((heads, tok, 1), f32), own_shape, *sends),
        (order, at, hide, queries, here, early, *out_list),
        [SM, SM] + [VM] * (4 + count),
        scratch=[pltpu.VMEM((count, tok, width), f32)],
    )
    got = tensor_exchange([None] + parts)
    mid, normed_chunk = call(
        mid_kernel, "mid", (own_shape, sends[0]),
        (at, block_in, by_slice(ffn_gain), by_slice(ffn_bias), own, *got),
        [SM] + [VM] * (4 + len(got)),
    )
    normed_two = tensor_gather(normed_chunk)

    hid_shape = shape((tok, hid), bf16)
    buffer = pltpu.VMEM((model, hid), bf16)
    two_kept, two_sent, hidden, gate_grad, up_grad, grad_own, *grad_parts = call(
        functools.partial(ffn_kernel, slots, peers), "ffn",
        (*slice_pair, hid_shape, hid_shape, hid_shape, own_shape, *sends),
        (order, *normed_two, cot, ffn_all), [SM] + [VM] * (peers + 1) + [HB],
        scratch=[buffer] * 3
        + [
            pltpu.SemaphoreType.DMA((3, count)), pltpu.VMEM((tok, model), bf16),
            pltpu.VMEM((tok, hid), f32),
        ],
    )
    got = tensor_exchange([None] + grad_parts)
    two_got, cot_got, hidden_got, gate_got, up_got = plane.across(
        (two_sent, cot_sent, hidden, gate_grad, up_grad)
    )
    place = jnp.stack([plane.rank(k) for k in plane.kept])
    of_slot = pl.BlockSpec((1, tok, width), lambda i, place: (i, 0, 0))
    whole = pl.BlockSpec((tok, hid), lambda i, place: (0, 0))
    ffn_grads = pl.pallas_call(
        ffn_weights_kernel,
        grid_spec=pltpu.PrefetchScalarGridSpec(
            num_scalar_prefetch=1,
            grid=(count // 2,),
            in_specs=[of_slot] * 4 + [whole] * 6,
            out_specs=pl.BlockSpec((3 * width, hid), lambda i, place: (place[i], 0)),
        ),
        out_shape=shape((count // 2 * 3 * width, hid), bf16),
        **params("ffn_weights"),
    )(
        place, two_kept, two_got, cot_kept, cot_got,
        gate_grad, gate_got, up_grad, up_got, hidden, hidden_got,
    )
    block_part = call(
        down_kernel, "down", shape((tok, model), bf16), (at, hidden, ffn_all, mid),
        [SM, VM, HB, VM], scratch=[buffer, pltpu.SemaphoreType.DMA((count,))],
    )
    block_out = lax.psum(block_part, "tensor")
    ffn_total = lax.psum_scatter(
        tie(ffn_grads, block_part),
        PLANE, scatter_dimension=0, axis_index_groups=plane.groups, tiled=True,
    )
    grad_own = tie(grad_own, ffn_grads, block_part)
    vec = shape((count, 1, width), f32)
    mid_grad, low_chunk, ffn_gain_grad, ffn_bias_grad = call(
        mid_back_kernel, "mid_back", (own_shape, sends[0], vec, vec),
        (mid, cot, by_slice(ffn_gain), grad_own, *got),
        [VM] * (4 + len(got)),
    )
    low_blocks = tensor_gather(low_chunk)

    low_kept, low_sent, dq, dhere, dearly = call(
        functools.partial(attend_back_kernel, slots, peers), "attend_back",
        (
            *slice_pair, shape((tok, feat), bf16),
            shape((2, tok, feat), f32), shape((2, tok, feat), bf16),
        ),
        (order, at, hide, tables, queries, here, early, logs, *low_blocks, *out_list),
        [SM, SM] + [VM] * (6 + peers + count),
        scratch=[pltpu.VMEM((tok, feat), bf16)],
    )
    dback = lax.ppermute(dearly, "context", [(i + 1, i) for i in range(plane.context - 1)])
    halves = (plane.halves(plane.down), plane.halves(plane.up))
    half = feat // 2
    stacks = lambda *dims: (shape((count // 4,) + dims, bf16),) * 4
    out_grads = call(
        functools.partial(out_weights_kernel, slots, halves), "out_weights", stacks(half, width),
        (attended, plane.across(attended), low_kept, plane.across(low_sent)), [VM] * 4,
    )
    out_a = Scatter(plane, *out_grads[:2], plane.down)
    out_b = Scatter(plane, *out_grads[2:], plane.up)
    out_total = [out_a.total(dback), out_b.total(dback)]
    results = call(
        functools.partial(one_grad_kernel, pieces), "one_grad",
        (
            *[shape((tok, feat), bf16)] * 3, shape((3, 1, feat), f32), vec, vec, own_shape, *sends,
        ),
        (order, at, block_in, tables, dq, dhere, dback, *qkv_list),
        [SM, SM] + [VM] * (5 + sum(pieces)),
        scratch=[pltpu.VMEM((count, tok, width), f32)],
    )
    back, (bias_grad, attn_gain_grad, attn_bias_grad, own), parts = (
        results[:3], results[3:7], results[7:]
    )
    got = tensor_exchange([None, *parts])
    qkv_grads = call(
        functools.partial(qkv_weights_kernel, slots, halves), "qkv_weights", stacks(3, width, half),
        (one_kept, plane.across(one_sent), *back, *plane.across(back)), [VM] * 8,
    )
    qkv_a = Scatter(plane, *qkv_grads[:2], plane.down)
    qkv_b = Scatter(plane, *qkv_grads[2:], plane.up)
    qkv_total = [qkv_a.total(out_total), qkv_b.total(out_total)]
    grad_chunk = call(
        input_grad_kernel, "input_grad", sends[0],
        (at, block_in, by_slice(attn_gain), mid_grad, own, *got),
        [SM] + [VM] * (4 + len(got)),
    )
    grad_blocks = tensor_gather(grad_chunk)
    input_grad = call(
        join_kernel, "input_grad_rows", shape((tok, model), bf16), (at, *grad_blocks),
        [SM] + [VM] * peers,
    )
    gate_up_grad, down_grad = call(
        ffn_out_kernel, "ffn_out", (shape((2, width, hid), f32), shape((hid, width), f32)),
        (ffn_total,), [VM],
    )

    small = jnp.concatenate(
        [
            v.reshape(-1)
            for v in (attn_gain_grad, attn_bias_grad, ffn_gain_grad, ffn_bias_grad, bias_grad)
        ]
    )
    small = plane.total(tie(small, got))
    vectors = small[: 4 * model].reshape(4, model)
    vectors = vectors + sum(tensor_swap(vectors, j) for j in range(1, peers))
    qkv_bias_grad = small[4 * model :].reshape(3, feat)

    return (
        block_out,
        input_grad,
        vectors[0],
        vectors[1],
        jnp.concatenate(qkv_total, axis=2),
        qkv_bias_grad,
        jnp.concatenate(out_total, axis=0),
        vectors[2],
        vectors[3],
        gate_up_grad,
        down_grad,
    )


def solution(mesh):
    in_specs = (
        P(("fsdp", "context"), None),
        P("fsdp", None),
        P(),
        P(),
        P(None, ("fsdp", "context"), "tensor"),
        P(None, "tensor"),
        P("tensor", ("fsdp", "context")),
        P(),
        P(),
        P(None, ("fsdp", "context"), "tensor"),
        P("tensor", ("fsdp", "context")),
        P(("fsdp", "context"), None),
    )
    out_specs = (
        P(("fsdp", "context"), None),
        P(("fsdp", "context"), None),
        P(),
        P(),
        P(None, ("fsdp", "context"), "tensor"),
        P(None, "tensor"),
        P("tensor", ("fsdp", "context")),
        P(),
        P(),
        P(None, ("fsdp", "context"), "tensor"),
        P("tensor", ("fsdp", "context")),
    )
    return jax.shard_map(
        on_device, mesh=mesh, in_specs=in_specs, out_specs=out_specs, check_vma=False
    )
```

```python
import functools
import math

import jax
import jax.numpy as jnp
from jax import lax
from jax.experimental import pallas as pl
from jax.experimental.pallas import tpu as pltpu
from jax.sharding import PartitionSpec as P

HD = 64
ROT = 16
EPS = 1e-05
NEG = -1e30
f32 = jnp.float32
bf16 = jnp.bfloat16
VM = pl.BlockSpec(memory_space=pltpu.VMEM)
SM = pl.BlockSpec(memory_space=pltpu.SMEM)
HB = pl.BlockSpec(memory_space=pl.ANY)
PLANE = ("fsdp", "context")


def shape(dims, dtype):
    return jax.ShapeDtypeStruct(tuple(dims), dtype)


WEIGHT = dict(
    norm_one=5, cotangent_rows=5, qkv=10, mid=250, mid_back=60, attend_back=200, block_out=5,
    input_grad=8, input_grad_rows=8,
)


def params(name):
    return dict(
        name=name,
        compiler_params=pltpu.CompilerParams(vmem_limit_bytes=56 * 2**20),
        cost_estimate=pl.CostEstimate(
            flops=int(1.15e9 * WEIGHT.get(name, 0)), bytes_accessed=0, transcendentals=0
        ),
    )


def call(kernel, name, outs, args, specs, scratch=()):
    return pl.pallas_call(
        kernel,
        out_shape=outs,
        in_specs=specs,
        out_specs=jax.tree.map(lambda _: VM, outs),
        scratch_shapes=list(scratch),
        **params(name),
    )(*args)


def dot(a, b, dims=((1,), (0,))):
    return lax.dot_general(a, b, (dims, ((), ())), preferred_element_type=f32)


NT = ((1,), (1,))
TN = ((0,), (0,))


def tie(value, *others):
    return lax.optimization_barrier((value, others))[0]


class Plane:
    def __init__(self):
        self.fsdp = lax.axis_size("fsdp")
        self.context = lax.axis_size("context")
        self.count = self.fsdp * self.context
        self.me = lax.axis_index("fsdp") * self.context + lax.axis_index("context")
        self.core = self.context
        bits = [1 << i for i in range(int(math.log2(self.count))) if (1 << i) != self.core]
        self.up, self.down = bits, bits[::-1]
        self.kept = [k for k in range(self.count) if not k & self.core]
        self.sent = [k ^ self.core for k in self.kept]
        own = [[d for d in range(self.count) if d & self.core == c] for c in (0, self.core)]
        self.groups = own

    def rank(self, k):
        low = self.core - 1
        squeeze = lambda d: (d & low) | ((d >> 1) & ~low)
        return squeeze(self.me) ^ squeeze(k)

    def swap(self, value, mask):
        pairs = [(i, i ^ mask) for i in range(self.count)]
        return lax.ppermute(value, ("fsdp", "context"), pairs)

    def across(self, value):
        return jax.tree.map(lambda v: self.swap(v, self.core), value)

    def gather(self, shard, *after):
        slots = {k: self.swap(shard, k) if k else shard for k in self.kept}
        for k in self.kept:
            value = tie(slots[k], after) if after and k == self.kept[-1] else slots[k]
            slots[k ^ self.core] = self.across(value)
        return slots

    def halves(self, order):
        slots = sorted(self.kept, key=lambda k: tuple(not k & bit for bit in order))
        return slots[: len(slots) // 2], slots[len(slots) // 2 :]

    def chip_total(self, value):
        for bit in self.up:
            value = value + self.swap(value, bit)
        return value


def scatter(plane, first, second, order):
    low, terms = first, [second]
    for bit in order:
        terms.append(plane.swap(low, bit))
        rest = terms[-1].shape[0] // 2
        if rest:
            pick = lambda t: t[t.shape[0] - 2 * rest :][:rest].astype(f32)
            low = sum(pick(t) for t in terms).astype(bf16)
    return terms


def tensor_swap(value, j):
    peers = lax.axis_size("tensor")
    return lax.ppermute(value, "tensor", [(i, i ^ j) for i in range(peers)])


def tensor_exchange(parts):
    return [tensor_swap(part, j) for j, part in enumerate(parts) if j]


def tensor_gather(part):
    return [part] + [tensor_swap(part, j) for j in range(1, lax.axis_size("tensor"))]


def row_stats(x3):
    size = x3.shape[0] * x3.shape[2]
    mean = jnp.sum(jnp.sum(x3, axis=0), axis=-1, keepdims=True) / size
    center = x3 - mean[None]
    var = jnp.sum(jnp.sum(center * center, axis=0), axis=-1, keepdims=True) / size
    inv = lax.rsqrt(var + EPS)
    return center * inv[None], inv


def row_mean(x3):
    return jnp.sum(jnp.sum(x3, axis=0), axis=-1, keepdims=True) / (x3.shape[0] * x3.shape[2])


def split(x, count):
    width = x.shape[1] // count
    return jnp.stack([x[:, i * width : (i + 1) * width] for i in range(count)])


def by_slot(slots, order_ref, from_ref, kept_ref, sent_ref):
    for ref, which in zip((kept_ref, sent_ref), slots):
        for i, k in enumerate(which):
            ref[i] = from_ref[order_ref[k]]


def norm_kernel(slots, order_ref, x_ref, gain_ref, bias_ref, kept_ref, sent_ref, normed):
    normal, _ = row_stats(split(x_ref[...].astype(f32), normed.shape[0]))
    normed[...] = (normal * gain_ref[...] + bias_ref[...]).astype(bf16)
    by_slot(slots, order_ref, normed, kept_ref, sent_ref)


def reorder_kernel(slots, order_ref, at_ref, x_ref, out_ref, kept_ref, sent_ref, slices):
    rows = x_ref.shape[0] // at_ref.shape[0]
    for j in range(at_ref.shape[0]):
        block = x_ref[pl.ds(pl.multiple_of(at_ref[j] * rows, rows), rows), :]
        out_ref[j * rows : (j + 1) * rows, :] = block
        slices[:, j * rows : (j + 1) * rows, :] = split(block, slices.shape[0])
    by_slot(slots, order_ref, slices, kept_ref, sent_ref)


def spin(x, tables, sign):
    parts = []
    for i in range(x.shape[1] // 128):
        v = x[:, i * 128 : (i + 1) * 128]
        turned = pltpu.roll(v, 128 - ROT // 2, 1) * tables[1] + pltpu.roll(v, ROT // 2, 1) * tables[2]
        parts.append(v * tables[0] + (turned if sign > 0 else -turned))
    return jnp.concatenate(parts, axis=1)


def qkv_kernel(slots, kept_ref, sent_ref, bias_ref, table_ref, *refs):
    weights, (q_ref, kv_ref) = refs[:-2], refs[-2:]
    feat = q_ref.shape[1]
    x = {k: ref[i] for ref, which in zip((kept_ref, sent_ref), slots) for i, k in enumerate(which)}
    for cols in tiles(feat):
        for j in range(3):
            total = bias_ref[j, :, cols]
            for k, weight in enumerate(weights):
                total = total + dot(x[k], weight[j, :, cols])
            if j < 2:
                total = spin(total, table_ref[...], 1)
            if j == 0:
                q_ref[:, cols] = total.astype(bf16)
            else:
                kv_ref[j - 1, :, cols] = total.astype(bf16)


def head_mask(rows, h):
    lane = lax.broadcasted_iota(jnp.int32, (rows, 2 * HD), 1)
    return (lane // HD) == h


def attend_kernel(count, order_ref, at_ref, hide_ref, q_ref, here_ref, early_ref, *refs):
    weights = refs[:count]
    att_ref, log_ref, own_ref = refs[count : count + 3]
    sends = refs[count + 3 : -1]
    part_ref = refs[-1]
    rows, feat = q_ref.shape
    scale = HD**-0.5
    for pair in range(feat // (2 * HD)):
        cols = slice(pair * 2 * HD, (pair + 1) * 2 * HD)
        q = q_ref[:, cols]
        k = jnp.concatenate([early_ref[0, :, cols], here_ref[0, :, cols]], axis=0)
        v = jnp.concatenate([early_ref[1, :, cols], here_ref[1, :, cols]], axis=0)
        out = []
        for h in range(2):
            mask = head_mask(rows, h)
            scores = dot(jnp.where(mask, q, 0), k, NT) * scale + hide_ref[...]
            top = jnp.max(scores, axis=-1, keepdims=True)
            exps = jnp.exp(scores - top)
            total = jnp.sum(exps, axis=-1, keepdims=True)
            log_ref[2 * pair + h] = top + jnp.log(total)
            out.append(dot((exps / total).astype(bf16), v))
        att_ref[:, cols] = jnp.where(head_mask(rows, 0), out[0], out[1]).astype(bf16)
    for k in range(count):
        part_ref[order_ref[k]] = dot(att_ref[...], weights[k][...])
    hand_out(at_ref, part_ref, own_ref, sends)


def hand_out(at_ref, part_ref, own_ref, sends):
    rows = own_ref.shape[1]
    for j in range(at_ref.shape[0]):
        block = part_ref[:, pl.ds(pl.multiple_of(at_ref[j] * rows, rows), rows), :]
        if j == 0:
            own_ref[...] = block
        else:
            sends[j - 1][...] = block.astype(bf16)


def ffn_out_kernel(total_ref, gate_up_ref, down_ref):
    width = down_ref.shape[1]
    for i in range(2):
        gate_up_ref[i] = total_ref[i * width : (i + 1) * width].astype(f32)
    down_ref[...] = total_ref[2 * width :].astype(f32).T


def mid_kernel(at_ref, x_ref, gain_ref, bias_ref, own_ref, *refs):
    mid_ref, normed_ref = refs[-2:]
    rows = own_ref.shape[1]
    total = own_ref[...]
    for ref in refs[:-2]:
        total = total + ref[...].astype(f32)
    block = x_ref[pl.ds(pl.multiple_of(at_ref[0] * rows, rows), rows), :].astype(f32)
    mid = split(block, own_ref.shape[0]) + total
    mid_ref[...] = mid
    normal, _ = row_stats(mid)
    normed_ref[...] = (normal * gain_ref[...] + bias_ref[...]).astype(bf16)


def pack_kernel(gate_up_ref, down_ref, out_ref):
    width = down_ref.shape[1]
    out_ref[:width] = gate_up_ref[0]
    out_ref[width : 2 * width] = gate_up_ref[1]
    out_ref[2 * width :] = down_ref[...].T


def fetch(all_ref, which, to_ref, sem):
    count, rows, _ = all_ref.shape
    width = rows // 3
    copies = [
        pltpu.make_async_copy(
            all_ref.at[n, pl.ds(which * width, width)], to_ref.at[pl.ds(n * width, width)], sem.at[n]
        )
        for n in range(count)
    ]
    for copy in copies:
        copy.start()
    return copies


def tiles(size, step=256):
    return [slice(i, min(i + step, size)) for i in range(0, size, step)]


def ffn_kernel(slots, peers, order_ref, *refs):
    blocks = refs[:peers]
    cot_ref, all_ref, kept_ref, sent_ref, three_ref, own_ref = refs[peers : peers + 6]
    gate_grad_ref, up_grad_ref, hidden_ref = (three_ref.at[i] for i in range(3))
    sends, (gate, up, down, sems, x_ref, pre_ref) = refs[peers + 6 : -6], refs[-6:]
    copies = [fetch(all_ref, i, ref, sems.at[i]) for i, ref in enumerate((gate, up, down))]
    rows, width = own_ref.shape[1:]
    for j, ref in enumerate(blocks):
        at = slice(j * rows, (j + 1) * rows)
        for n in range(own_ref.shape[0]):
            x_ref[at, n * width : (n + 1) * width] = ref[n]
        for to_ref, which in zip((kept_ref, sent_ref), slots):
            for i, k in enumerate(which):
                to_ref[i, at, :] = ref[order_ref[k]]
    x = x_ref[...]
    for copy in copies[0]:
        copy.wait()
    for cols in tiles(hidden_ref.shape[1]):
        pre_ref[:, cols] = dot(x, gate[:, cols])
    for copy in copies[1] + copies[2]:
        copy.wait()
    for cols in tiles(hidden_ref.shape[1]):
        gate_pre = pre_ref[:, cols]
        up_pre = dot(x, up[:, cols])
        hidden_grad = dot(cot_ref[...], down[:, cols])
        sigma = 1.0 / (1.0 + jnp.exp(-gate_pre))
        silu = gate_pre * sigma
        hidden_ref[:, cols] = (silu * up_pre).astype(bf16)
        gate_grad_ref[:, cols] = (
            hidden_grad * up_pre * sigma * (1.0 + gate_pre * (1.0 - sigma))
        ).astype(bf16)
        up_grad_ref[:, cols] = (hidden_grad * silu).astype(bf16)
    for n in range(own_ref.shape[0]):
        at = slice(n * width, (n + 1) * width)
        total = dot(gate_grad_ref[...], gate[at], NT) + dot(up_grad_ref[...], up[at], NT)
        cut(n, total, own_ref, sends)


def cut(n, total, own_ref, sends):
    rows = own_ref.shape[1]
    own_ref[n] = total[:rows]
    for j, ref in enumerate(sends):
        ref[n] = total[(j + 1) * rows : (j + 2) * rows].astype(bf16)


def down_kernel(three_ref, all_ref, own_ref, *refs):
    sends, (down, sem) = refs[:-2], refs[-2:]
    hidden_ref = three_ref.at[2]
    for copy in fetch(all_ref, 2, down, sem):
        copy.wait()
    count, _, width = own_ref.shape
    for n in range(count):
        cut(n, dot(hidden_ref[...], down[n * width : (n + 1) * width], NT), own_ref, sends)


def block_out_kernel(mid_ref, own_ref, *refs):
    total = mid_ref[...] + own_ref[...]
    for ref in refs[:-1]:
        total = total + ref[...].astype(f32)
    refs[-1][...] = total.astype(bf16)


def ffn_weights_kernel(place_ref, *refs):
    x, cot, grads, out_ref = refs[:2], refs[2:4], refs[4:6], refs[6]
    width = x[0].shape[2]
    for i, left in enumerate((x, x, cot)):
        total = dot(left[0][0], grads[0][i], TN) + dot(left[1][0], grads[1][i], TN)
        out_ref[i * width : (i + 1) * width] = total.astype(bf16)


def norm_back(normal, inv, grad, gain):
    scaled = grad * gain
    inner = row_mean(scaled * normal)
    return inv[None] * (scaled - row_mean(scaled)[None] - normal * inner[None])


def token_sum(x3):
    return jnp.sum(x3, axis=1, keepdims=True)


def mid_back_kernel(mid_ref, cot_ref, gain_ref, own_ref, *refs):
    grad_ref, low_ref, gain_grad_ref, bias_grad_ref = refs[-4:]
    total = own_ref[...]
    for ref in refs[:-4]:
        total = total + ref[...].astype(f32)
    normal, inv = row_stats(mid_ref[...])
    gain_grad_ref[...] = token_sum(total * normal)
    bias_grad_ref[...] = token_sum(total)
    cot = split(cot_ref[: mid_ref.shape[1]].astype(f32), mid_ref.shape[0])
    grad = cot + norm_back(normal, inv, total, gain_ref[...])
    grad_ref[...] = grad
    low_ref[...] = grad.astype(bf16)


def attend_back_kernel(
    slots, peers, order_ref, at_ref, hide_ref, table_ref, q_ref, here_ref, early_ref, log_ref, *refs
):
    count = order_ref.shape[0]
    lows = refs[:peers]
    weights = refs[peers : peers + count]
    kept_ref, sent_ref, dq_ref, dhere_ref, dearly_ref, datt = refs[peers + count :]
    rows, feat = q_ref.shape
    part = rows // peers
    scale = HD**-0.5
    low = {}
    for ref, which in zip((kept_ref, sent_ref), slots):
        for i, k in enumerate(which):
            low[k] = ref.at[i]
            for j in range(peers):
                at = pl.ds(pl.multiple_of(at_ref[j] * part, part), part)
                ref[i, at, :] = lows[j][order_ref[k]]
    for cols in tiles(feat):
        total = dot(low[0][...], weights[0][cols], NT)
        for k in range(1, count):
            total = total + dot(low[k][...], weights[k][cols], NT)
        datt[:, cols] = total.astype(bf16)
    for pair in range(feat // (2 * HD)):
        cols = slice(pair * 2 * HD, (pair + 1) * 2 * HD)
        q = q_ref[:, cols]
        k = jnp.concatenate([early_ref[0, :, cols], here_ref[0, :, cols]], axis=0)
        v = jnp.concatenate([early_ref[1, :, cols], here_ref[1, :, cols]], axis=0)
        da = datt[:, cols]
        grads = []
        for h in range(2):
            mask = head_mask(rows, h)
            scores = dot(jnp.where(mask, q, 0), k, NT) * scale + hide_ref[...]
            probs = jnp.exp(scores - log_ref[2 * pair + h])
            weight_grad = dot(jnp.where(mask, da, 0), v, NT)
            inner = jnp.sum(probs * weight_grad, axis=-1, keepdims=True)
            score_grad = (probs * (weight_grad - inner)).astype(bf16)
            grads.append(
                (
                    dot(score_grad, k) * scale,
                    dot(score_grad, q, TN) * scale,
                    dot(probs.astype(bf16), da, TN),
                )
            )
        dq = jnp.where(head_mask(rows, 0), grads[0][0], grads[1][0])
        dq_ref[:, cols] = spin(dq, table_ref[...], -1).astype(bf16)
        for i in (1, 2):
            both = jnp.where(head_mask(2 * rows, 0), grads[0][i], grads[1][i])
            dearly_ref[i - 1, :, cols] = both[:rows].astype(bf16)
            dhere_ref[i - 1, :, cols] = both[rows:]


def one_grad_kernel(
    order_ref, at_ref, x_ref, table_ref, dq_ref, dhere_ref, dback_ref, *refs
):
    count = order_ref.shape[0]
    weights, refs = refs[:count], refs[count:]
    ffn_gain_ref, ffn_bias_ref, back_ref, small_ref, own_ref = refs[:5]
    sends, part_ref = refs[5:-1], refs[-1]
    width = own_ref.shape[2]
    back_refs = [back_ref.at[j] for j in range(3)]
    back_refs[0][...] = dq_ref[...]
    dk = dhere_ref[0] + dback_ref[0].astype(f32)
    back_refs[1][...] = spin(dk, table_ref[...], -1).astype(bf16)
    back_refs[2][...] = (dhere_ref[1] + dback_ref[1].astype(f32)).astype(bf16)
    row = 4 * count
    for ref in back_refs:
        bias = jnp.sum(ref[...].astype(f32), axis=0, keepdims=True)
        for at in range(0, ref.shape[1], width):
            small_ref[row : row + 1] = bias[:, at : at + width]
            row += 1
    for k, weight in enumerate(weights):
        part_ref[order_ref[k]] = sum(dot(ref[...], weight[j], NT) for j, ref in enumerate(back_refs))
    normal, _ = row_stats(split(x_ref[...].astype(f32), count))
    small_ref[:count] = token_sum(part_ref[...] * normal)[:, 0]
    small_ref[count : 2 * count] = token_sum(part_ref[...])[:, 0]
    small_ref[2 * count : 3 * count] = ffn_gain_ref[:, 0]
    small_ref[3 * count : 4 * count] = ffn_bias_ref[:, 0]
    hand_out(at_ref, part_ref, own_ref, sends)


def attention_weights_kernel(slots, halves, *refs):
    x, back, low, att, outs = refs[:2], refs[2:4], refs[4:6], refs[6:8], refs[8:]
    part = att[0].shape[1] // 2
    for h, both in enumerate(halves):
        cols = slice(h * part, (h + 1) * part)
        for ref, which in zip(outs[2 * h :], both):
            for i, k in enumerate(which):
                at = slots[0].index(k)
                for j in range(4):
                    left = x if j < 3 else low
                    right = [b[j, :, cols] for b in back] if j < 3 else [a[:, cols] for a in att]
                    total = dot(left[0][at], right[0], TN) + dot(left[1][at], right[1], TN)
                    ref[i, j] = total.astype(bf16)


def attention_out_kernel(terms, *refs):
    qkv_ref, out_ref = refs[-2:]
    part = qkv_ref.shape[2] // 2
    for h in range(2):
        cols = slice(h * part, (h + 1) * part)
        for j in range(4):
            total = sum(ref[ref.shape[0] - 1, j].astype(f32) for ref in refs[h * terms : (h + 1) * terms])
            if j < 3:
                qkv_ref[j, :, cols] = total
            else:
                out_ref[cols, :] = total.T


def input_grad_kernel(at_ref, x_ref, gain_ref, mid_grad_ref, own_ref, small_ref, *refs):
    parts, out_ref = refs[:-1], refs[-1]
    count, rows, width = own_ref.shape
    total = own_ref[...]
    for ref in parts:
        total = total + ref[...].astype(f32)
    block = x_ref[pl.ds(pl.multiple_of(at_ref[0] * rows, rows), rows), :].astype(f32)
    normal, inv = row_stats(split(block, count))
    grad = mid_grad_ref[...] + norm_back(normal, inv, total, gain_ref[...])
    out_ref[: count * rows] = grad.astype(bf16).reshape(count * rows, width)
    out_ref[count * rows :] = small_ref[: 4 * count].astype(bf16)


def join_kernel(at_ref, *refs):
    out_ref = refs[-1]
    slices, rows, width = refs[0].shape
    for j, ref in enumerate(refs[:-1]):
        at = pl.ds(pl.multiple_of(at_ref[j] * rows, rows), rows)
        for n in range(slices):
            out_ref[at, n * width : (n + 1) * width] = ref[n]


def join_grad_kernel(at_ref, small_ref, *refs):
    blocks, (out_ref, total_ref) = refs[:-2], refs[-2:]
    width = small_ref.shape[1]
    count = out_ref.shape[1] // width
    rows = out_ref.shape[0] // len(blocks)
    total_ref[...] = small_ref[...]
    for j, ref in enumerate(blocks):
        at = pl.ds(pl.multiple_of(at_ref[j] * rows, rows), rows)
        for n in range(count):
            out_ref[at, n * width : (n + 1) * width] = ref[n * rows : (n + 1) * rows]
        if j:
            total_ref[: 4 * count] += ref[count * rows :].astype(f32)


def on_device(
    block_in,
    seq_lengths,
    attn_gain,
    attn_bias,
    qkv_weight,
    qkv_bias,
    out_weight,
    ffn_gain,
    ffn_bias,
    gate_up_weight,
    down_weight,
    out_cotangent,
):
    tok, model = block_in.shape
    feat = qkv_weight.shape[2]
    hid = down_weight.shape[0]
    plane = Plane()
    count = plane.count
    width = model // count
    peers = lax.axis_size("tensor")
    chunk = tok // peers
    heads = feat // HD
    order = plane.me ^ jnp.arange(count, dtype=jnp.int32)
    at = lax.axis_index("tensor") ^ jnp.arange(peers, dtype=jnp.int32)

    offset = lax.axis_index("context") * tok
    places = offset + jnp.arange(tok, dtype=jnp.int32)
    lengths = seq_lengths[0]
    ends = jnp.cumsum(lengths)
    starts = jnp.sum(jnp.where(ends[None, :] <= places[:, None], lengths[None, :], 0), axis=1)
    turn = ROT // 2
    frequency = jnp.exp(jnp.arange(turn).astype(f32) * (-2.0 * math.log(10000.0) / ROT))
    angles = (places - starts).astype(f32)[:, None] * frequency[None, :]
    cosine = jnp.tile(jnp.cos(angles), (1, 128 // turn))
    sine = jnp.tile(jnp.sin(angles), (1, 128 // turn))
    lane = jnp.arange(128)[None, :] % HD
    tables = jnp.stack(
        [
            jnp.where(lane < ROT, cosine, 1.0),
            jnp.where(lane < turn, -sine, 0.0),
            jnp.where((lane >= turn) & (lane < ROT), sine, 0.0),
        ]
    )
    key_places = offset - tok + jnp.arange(2 * tok, dtype=jnp.int32)
    visible = (key_places[None, :] <= places[:, None]) & (key_places[None, :] >= starts[:, None])
    hide = jnp.where(visible, 0.0, NEG).astype(f32)

    by_slice = lambda vec: vec.reshape(count, 1, width)
    slots = (plane.kept, plane.sent)
    slice_pair = (shape((count // 2, tok, width), bf16),) * 2
    slices = pltpu.VMEM((count, tok, width), bf16)
    one_kept, one_sent = call(
        functools.partial(norm_kernel, slots), "norm_one", slice_pair,
        (order, block_in, by_slice(attn_gain), by_slice(attn_bias)), [SM] + [VM] * 3,
        scratch=[slices],
    )
    cot, cot_kept, cot_sent = call(
        functools.partial(reorder_kernel, slots), "cotangent_rows",
        (shape((tok, model), bf16), *slice_pair), (order, at, out_cotangent), [SM, SM, VM],
        scratch=[slices],
    )

    qkv_slots = plane.gather(qkv_weight)
    qkv_list = [qkv_slots[k] for k in range(count)]
    ffn_shard = call(
        pack_kernel, "ffn_shard", shape((3 * width, hid), bf16), (gate_up_weight, down_weight),
        [VM, VM],
    )
    out_slots = plane.gather(tie(out_weight, ffn_shard))
    out_list = [out_slots[k] for k in range(count)]
    first = (qkv_slots[plane.up[0]], qkv_slots[plane.up[-1]])
    ffn_all = lax.all_gather(tie(ffn_shard, first), PLANE, axis=0, tiled=False)

    queries, here = call(
        functools.partial(qkv_kernel, slots), "qkv",
        (shape((tok, feat), bf16), shape((2, tok, feat), bf16)),
        (one_kept, one_sent, qkv_bias.reshape(3, 1, feat), tables, *qkv_list),
        [VM] * (4 + count),
    )
    early = lax.ppermute(here, "context", [(i, i + 1) for i in range(plane.context - 1)])
    sends = [shape((count, chunk, width), bf16)] * (peers - 1)
    own_shape = shape((count, chunk, width), f32)
    attended, logs, own, *parts = call(
        functools.partial(attend_kernel, count), "attend",
        (shape((tok, feat), bf16), shape((heads, tok, 1), f32), own_shape, *sends),
        (order, at, hide, queries, here, early, *out_list),
        [SM, SM] + [VM] * (4 + count),
        scratch=[pltpu.VMEM((count, tok, width), f32)],
    )
    got = tensor_exchange([None] + parts)
    cot_got, one_got, att_got = plane.across((cot_sent, one_sent, attended))
    own = tie(own, cot_got, one_got, att_got)
    mid, normed_chunk = call(
        mid_kernel, "mid", (own_shape, sends[0]),
        (at, block_in, by_slice(ffn_gain), by_slice(ffn_bias), own, *got),
        [SM] + [VM] * (4 + len(got)),
    )
    normed_two = tensor_gather(normed_chunk)

    buffer = pltpu.VMEM((model, hid), bf16)
    two_kept, two_sent, three, grad_own, *grad_parts = call(
        functools.partial(ffn_kernel, slots, peers), "ffn",
        (*slice_pair, shape((3, tok, hid), bf16), own_shape, *sends),
        (order, *normed_two, cot, ffn_all), [SM] + [VM] * (peers + 1) + [HB],
        scratch=[buffer] * 3
        + [
            pltpu.SemaphoreType.DMA((3, count)), pltpu.VMEM((tok, model), bf16),
            pltpu.VMEM((tok, hid), f32),
        ],
    )
    got = tensor_exchange([None] + grad_parts)
    two_got, three_got = plane.across((two_sent, three))
    place = jnp.stack([plane.rank(k) for k in plane.kept])
    of_slot = pl.BlockSpec((1, tok, width), lambda i, place: (i, 0, 0))
    whole = pl.BlockSpec((3, tok, hid), lambda i, place: (0, 0, 0))
    ffn_grads = pl.pallas_call(
        ffn_weights_kernel,
        grid_spec=pltpu.PrefetchScalarGridSpec(
            num_scalar_prefetch=1,
            grid=(count // 2,),
            in_specs=[of_slot] * 4 + [whole] * 2,
            out_specs=pl.BlockSpec((3 * width, hid), lambda i, place: (place[i], 0)),
        ),
        out_shape=shape((count // 2 * 3 * width, hid), bf16),
        **params("ffn_weights"),
    )(place, two_kept, two_got, cot_kept, cot_got, three, three_got)
    down_own, *down_parts = call(
        down_kernel, "down", (own_shape, *sends), (three, ffn_all), [VM, HB],
        scratch=[buffer, pltpu.SemaphoreType.DMA((count,))],
    )
    ffn_total = lax.psum_scatter(
        ffn_grads, PLANE, scatter_dimension=0, axis_index_groups=plane.groups, tiled=True
    )
    grad_own = tie(grad_own, ffn_grads, down_own)
    vec = shape((count, 1, width), f32)
    mid_grad, low_chunk, ffn_gain_grad, ffn_bias_grad = call(
        mid_back_kernel, "mid_back", (own_shape, sends[0], vec, vec),
        (mid, cot, by_slice(ffn_gain), grad_own, *got),
        [VM] * (4 + len(got)),
    )
    low_blocks = tensor_gather(low_chunk)
    down_got = tensor_exchange([None, *tie(down_parts, low_blocks)])
    out_chunk = call(
        block_out_kernel, "block_out", sends[0], (mid, down_own, *down_got),
        [VM] * (2 + len(down_got)),
    )
    out_blocks = tensor_gather(out_chunk)

    low_kept, low_sent, dq, dhere, dearly = call(
        functools.partial(attend_back_kernel, slots, peers), "attend_back",
        (
            *slice_pair, shape((tok, feat), bf16),
            shape((2, tok, feat), f32), shape((2, tok, feat), bf16),
        ),
        (order, at, hide, tables, queries, here, early, logs, *low_blocks, *out_list),
        [SM, SM] + [VM] * (6 + peers + count),
        scratch=[pltpu.VMEM((tok, feat), bf16)],
    )
    low_got = plane.across(low_sent)
    dback = lax.ppermute(dearly, "context", [(i + 1, i) for i in range(plane.context - 1)])
    small_shape = shape((4 * count + 3 * feat // width, width), f32)
    back, small, own, *parts = call(
        one_grad_kernel, "one_grad",
        (
            shape((3, tok, feat), bf16), small_shape, own_shape, *sends,
        ),
        (
            order, at, block_in, tables, dq, tie(dhere, out_blocks, low_got), dback, *qkv_list,
            ffn_gain_grad, ffn_bias_grad,
        ),
        [SM, SM] + [VM] * (7 + count),
        scratch=[pltpu.VMEM((count, tok, width), f32)],
    )
    got = tensor_exchange([None, *parts])
    halves = (plane.halves(plane.down), plane.halves(plane.up))
    back_got = plane.across(back)
    small = plane.chip_total(small)
    weight_grads = call(
        functools.partial(attention_weights_kernel, slots, halves), "attention_weights",
        (shape((count // 4, 4, width, feat // 2), bf16),) * 4,
        (one_kept, one_got, tie(back, small), back_got, low_kept, low_got, attended, att_got), [VM] * 8,
    )
    terms_a = scatter(plane, *weight_grads[:2], plane.down)
    terms_b = scatter(plane, *weight_grads[2:], plane.up)
    grad_chunk = call(
        input_grad_kernel, "input_grad", shape((count * chunk + 4 * count, width), bf16),
        (at, block_in, by_slice(attn_gain), mid_grad, own, small, *got),
        [SM] + [VM] * (5 + len(got)),
    )
    grad_blocks = tensor_gather(grad_chunk)
    gate_up_grad, down_grad = call(
        ffn_out_kernel, "ffn_out", (shape((2, width, hid), f32), shape((hid, width), f32)),
        (ffn_total,), [VM],
    )
    block_out = call(
        join_kernel, "block_out_rows", shape((tok, model), bf16), (at, *out_blocks),
        [SM] + [VM] * peers,
    )
    input_grad, small = call(
        join_grad_kernel, "input_grad_rows", (shape((tok, model), bf16), small_shape),
        (at, small, *tie(grad_blocks, block_out, down_grad)), [SM] + [VM] * (1 + peers),
    )

    terms = (*terms_a, *terms_b)
    qkv_grad, out_grad = call(
        functools.partial(attention_out_kernel, len(terms_a)), "attention_out",
        (shape((3, width, feat), f32), shape((feat, width), f32)), terms, [VM] * len(terms),
    )
    small = small + plane.across(small)
    vectors = small[: 4 * count].reshape(4, model)
    return (
        block_out,
        input_grad,
        vectors[0],
        vectors[1],
        qkv_grad,
        small[4 * count :].reshape(3, feat),
        out_grad,
        vectors[2],
        vectors[3],
        gate_up_grad,
        down_grad,
    )


def solution(mesh):
    in_specs = (
        P(("fsdp", "context"), None),
        P("fsdp", None),
        P(),
        P(),
        P(None, ("fsdp", "context"), "tensor"),
        P(None, "tensor"),
        P("tensor", ("fsdp", "context")),
        P(),
        P(),
        P(None, ("fsdp", "context"), "tensor"),
        P("tensor", ("fsdp", "context")),
        P(("fsdp", "context"), None),
    )
    out_specs = (
        P(("fsdp", "context"), None),
        P(("fsdp", "context"), None),
        P(),
        P(),
        P(None, ("fsdp", "context"), "tensor"),
        P(None, "tensor"),
        P("tensor", ("fsdp", "context")),
        P(),
        P(),
        P(None, ("fsdp", "context"), "tensor"),
        P("tensor", ("fsdp", "context")),
    )
    return jax.shard_map(
        on_device, mesh=mesh, in_specs=in_specs, out_specs=out_specs, check_vma=False
    )
```

```python
import functools
import math

import jax
import jax.numpy as jnp
from jax import lax
from jax.experimental import pallas as pl
from jax.experimental.pallas import tpu as pltpu
from jax.sharding import PartitionSpec as P

HD = 64
ROT = 16
EPS = 1e-05
NEG = -1e30
f32 = jnp.float32
bf16 = jnp.bfloat16
VM = pl.BlockSpec(memory_space=pltpu.VMEM)
SM = pl.BlockSpec(memory_space=pltpu.SMEM)
HB = pl.BlockSpec(memory_space=pl.ANY)
PLANE = ("fsdp", "context")


def shape(dims, dtype):
    return jax.ShapeDtypeStruct(tuple(dims), dtype)


WEIGHT = dict(
    norm_one=5, cotangent_rows=5, qkv=10, mid=250, mid_back=60, attend_back=200, block_out=5,
    input_grad=8, input_grad_rows=8,
)


VMEM = dict(one_grad=32, attention_weights=24, input_grad=24, input_grad_rows=24, outputs=24)


def params(name):
    return dict(
        name=name,
        compiler_params=pltpu.CompilerParams(vmem_limit_bytes=VMEM.get(name, 56) * 2**20),
        cost_estimate=pl.CostEstimate(
            flops=int(1.15e9 * WEIGHT.get(name, 0)), bytes_accessed=0, transcendentals=0
        ),
    )


def call(kernel, name, outs, args, specs, scratch=()):
    return pl.pallas_call(
        kernel,
        out_shape=outs,
        in_specs=specs,
        out_specs=jax.tree.map(lambda _: VM, outs),
        scratch_shapes=list(scratch),
        **params(name),
    )(*args)


def dot(a, b, dims=((1,), (0,))):
    return lax.dot_general(a, b, (dims, ((), ())), preferred_element_type=f32)


NT = ((1,), (1,))
TN = ((0,), (0,))


def tie(value, *others):
    return lax.optimization_barrier((value, others))[0]


class Plane:
    def __init__(self):
        self.fsdp = lax.axis_size("fsdp")
        self.context = lax.axis_size("context")
        self.count = self.fsdp * self.context
        self.me = lax.axis_index("fsdp") * self.context + lax.axis_index("context")
        self.core = self.context
        bits = [1 << i for i in range(int(math.log2(self.count))) if (1 << i) != self.core]
        self.up, self.down = bits, bits[::-1]
        self.kept = [k for k in range(self.count) if not k & self.core]
        self.sent = [k ^ self.core for k in self.kept]
        own = [[d for d in range(self.count) if d & self.core == c] for c in (0, self.core)]
        self.groups = own

    def rank(self, k):
        low = self.core - 1
        squeeze = lambda d: (d & low) | ((d >> 1) & ~low)
        return squeeze(self.me) ^ squeeze(k)

    def swap(self, value, mask):
        pairs = [(i, i ^ mask) for i in range(self.count)]
        return lax.ppermute(value, ("fsdp", "context"), pairs)

    def across(self, value):
        return jax.tree.map(lambda v: self.swap(v, self.core), value)

    def gather(self, shard, *after):
        slots = {k: self.swap(shard, k) if k else shard for k in self.kept}
        for k in self.kept:
            value = tie(slots[k], after) if after and k == self.kept[-1] else slots[k]
            slots[k ^ self.core] = self.across(value)
        return slots

    def near(self, shard):
        return {0: shard} | {bit: self.swap(shard, bit) for bit in self.up}

    def pass_on(self, slots, *after):
        first = tie(slots[self.up[0]], after)
        slots = dict(slots)
        for k in self.kept:
            if k not in slots:
                source = k & -k
                value = first if source == self.up[0] else slots[source]
                slots[k] = self.swap(value, k ^ source)
        return slots | {k ^ self.core: self.across(v) for k, v in slots.items()}

    def halves(self, order):
        slots = sorted(self.kept, key=lambda k: tuple(not k & bit for bit in order))
        return slots[: len(slots) // 2], slots[len(slots) // 2 :]

    def chip_total(self, value):
        for bit in self.up:
            value = value + self.swap(value, bit)
        return value


def scatter(plane, first, second, order):
    low, terms = first, [second]
    for bit in order:
        terms.append(plane.swap(low, bit))
        rest = terms[-1].shape[0] // 2
        if rest:
            pick = lambda t: t[t.shape[0] - 2 * rest :][:rest].astype(f32)
            low = sum(pick(t) for t in terms).astype(bf16)
    return terms


def tensor_swap(value, j):
    peers = lax.axis_size("tensor")
    return lax.ppermute(value, "tensor", [(i, i ^ j) for i in range(peers)])


def tensor_exchange(parts):
    return [tensor_swap(part, j) for j, part in enumerate(parts) if j]


def tensor_gather(part):
    return [part] + [tensor_swap(part, j) for j in range(1, lax.axis_size("tensor"))]


def row_stats(x3):
    size = x3.shape[0] * x3.shape[2]
    mean = jnp.sum(jnp.sum(x3, axis=0), axis=-1, keepdims=True) / size
    center = x3 - mean[None]
    var = jnp.sum(jnp.sum(center * center, axis=0), axis=-1, keepdims=True) / size
    inv = lax.rsqrt(var + EPS)
    return center * inv[None], inv


def row_mean(x3):
    return jnp.sum(jnp.sum(x3, axis=0), axis=-1, keepdims=True) / (x3.shape[0] * x3.shape[2])


def split(x, count):
    width = x.shape[1] // count
    return jnp.stack([x[:, i * width : (i + 1) * width] for i in range(count)])


def by_slot(slots, order_ref, from_ref, kept_ref, sent_ref):
    for ref, which in zip((kept_ref, sent_ref), slots):
        for i, k in enumerate(which):
            ref[i] = from_ref[order_ref[k]]


def norm_kernel(
    slots, order_ref, at_ref, x_ref, gain_ref, bias_ref, flat_ref, kept_ref, sent_ref, chunk_ref, normed
):
    count, _, width = normed.shape
    rows = chunk_ref.shape[0]
    chunk_ref[...] = x_ref[pl.ds(pl.multiple_of(at_ref[0] * rows, rows), rows), :]
    normal, _ = row_stats(split(x_ref[...].astype(f32), count))
    normed[...] = (normal * gain_ref[...] + bias_ref[...]).astype(bf16)
    by_slot(slots, order_ref, normed, kept_ref, sent_ref)
    for k in range(count):
        flat_ref[:, k * width : (k + 1) * width] = normed[order_ref[k]]


def reorder_kernel(slots, order_ref, at_ref, x_ref, out_ref, kept_ref, sent_ref, chunk_ref, slices):
    rows = x_ref.shape[0] // at_ref.shape[0]
    chunk_ref[...] = x_ref[pl.ds(pl.multiple_of(at_ref[0] * rows, rows), rows), :]
    for j in range(at_ref.shape[0]):
        block = x_ref[pl.ds(pl.multiple_of(at_ref[j] * rows, rows), rows), :]
        out_ref[j * rows : (j + 1) * rows, :] = block
        slices[:, j * rows : (j + 1) * rows, :] = split(block, slices.shape[0])
    by_slot(slots, order_ref, slices, kept_ref, sent_ref)


def spin(x, tables, sign):
    parts = []
    for i in range(x.shape[1] // 128):
        v = x[:, i * 128 : (i + 1) * 128]
        turned = pltpu.roll(v, 128 - ROT // 2, 1) * tables[1] + pltpu.roll(v, ROT // 2, 1) * tables[2]
        parts.append(v * tables[0] + (turned if sign > 0 else -turned))
    return jnp.concatenate(parts, axis=1)


def qkv_kernel(x_ref, bias_ref, table_ref, *refs):
    weights, (q_ref, kv_ref) = refs[:-2], refs[-2:]
    feat, width = q_ref.shape[1], weights[0].shape[1]
    for cols in tiles(feat):
        for j in range(3):
            total = bias_ref[j, :, cols]
            for k, weight in enumerate(weights):
                total = total + dot(x_ref[:, k * width : (k + 1) * width], weight[j, :, cols])
            if j < 2:
                total = spin(total, table_ref[...], 1)
            if j == 0:
                q_ref[:, cols] = total.astype(bf16)
            else:
                kv_ref[j - 1, :, cols] = total.astype(bf16)


def head_mask(rows, h):
    lane = lax.broadcasted_iota(jnp.int32, (rows, 2 * HD), 1)
    return (lane // HD) == h


def attend_kernel(count, order_ref, at_ref, hide_ref, q_ref, here_ref, early_ref, *refs):
    weights = refs[:count]
    att_ref, log_ref, own_ref = refs[count : count + 3]
    sends = refs[count + 3 : -1]
    part_ref = refs[-1]
    rows, feat = q_ref.shape
    scale = HD**-0.5
    for pair in range(feat // (2 * HD)):
        cols = slice(pair * 2 * HD, (pair + 1) * 2 * HD)
        q = q_ref[:, cols] * scale
        out = []
        for h in range(2):
            mine = jnp.where(head_mask(rows, h), q, 0)
            first = dot(mine, early_ref[0, :, cols], NT) + hide_ref[:, :rows]
            second = dot(mine, here_ref[0, :, cols], NT) + hide_ref[:, rows:]
            top = jnp.max(jnp.maximum(first, second), axis=-1, keepdims=True)
            first, second = jnp.exp(first - top), jnp.exp(second - top)
            total = jnp.sum(first + second, axis=-1, keepdims=True)
            log_ref[2 * pair + h] = top + jnp.log(total)
            mixed = dot(first.astype(bf16), early_ref[1, :, cols])
            mixed = mixed + dot(second.astype(bf16), here_ref[1, :, cols])
            out.append(mixed * (1.0 / total))
        att_ref[:, cols] = jnp.where(head_mask(rows, 0), out[0], out[1]).astype(bf16)
    for k in range(count):
        part_ref[order_ref[k]] = dot(att_ref[...], weights[k][...])
    hand_out(at_ref, part_ref, own_ref, sends)


def hand_out(at_ref, part_ref, own_ref, sends):
    rows = own_ref.shape[1]
    for j in range(at_ref.shape[0]):
        block = part_ref[:, pl.ds(pl.multiple_of(at_ref[j] * rows, rows), rows), :]
        if j == 0:
            own_ref[...] = block
        else:
            sends[j - 1][...] = block.astype(bf16)


def ffn_out_kernel(total_ref, gate_up_ref, down_ref):
    width = down_ref.shape[1]
    for i in range(2):
        gate_up_ref[i] = total_ref[i * width : (i + 1) * width].astype(f32)
    down_ref[...] = total_ref[2 * width :].astype(f32).T


def mid_kernel(x_ref, gain_ref, bias_ref, own_ref, *refs):
    mid_ref, normed_ref = refs[-2:]
    total = own_ref[...]
    for ref in refs[:-2]:
        total = total + ref[...].astype(f32)
    mid = split(x_ref[...].astype(f32), own_ref.shape[0]) + total
    mid_ref[...] = mid
    normal, _ = row_stats(mid)
    normed_ref[...] = (normal * gain_ref[...] + bias_ref[...]).astype(bf16)


def pack_kernel(gate_up_ref, down_ref, out_ref):
    width = down_ref.shape[1]
    out_ref[:width] = gate_up_ref[0]
    out_ref[width : 2 * width] = gate_up_ref[1]
    out_ref[2 * width :] = down_ref[...].T


def fetch(all_ref, which, to_ref, sem):
    count, rows, _ = all_ref.shape
    width = rows // 3
    copies = [
        pltpu.make_async_copy(
            all_ref.at[n, pl.ds(which * width, width)], to_ref.at[pl.ds(n * width, width)], sem.at[n]
        )
        for n in range(count)
    ]
    for copy in copies:
        copy.start()
    return copies


def tiles(size, step=256):
    return [slice(i, min(i + step, size)) for i in range(0, size, step)]


def ffn_kernel(slots, peers, order_ref, *refs):
    blocks = refs[:peers]
    cot_ref, all_ref, kept_ref, sent_ref, three_ref, own_ref = refs[peers : peers + 6]
    gate_grad_ref, up_grad_ref, hidden_ref = (three_ref.at[i] for i in range(3))
    sends, (gate, up, down, sems, x_ref, pre_ref) = refs[peers + 6 : -6], refs[-6:]
    copies = [fetch(all_ref, i, ref, sems.at[i]) for i, ref in enumerate((gate, up, down))]
    rows, width = own_ref.shape[1:]
    for j, ref in enumerate(blocks):
        at = slice(j * rows, (j + 1) * rows)
        for n in range(own_ref.shape[0]):
            x_ref[at, n * width : (n + 1) * width] = ref[n]
        for to_ref, which in zip((kept_ref, sent_ref), slots):
            for i, k in enumerate(which):
                to_ref[i, at, :] = ref[order_ref[k]]
    x = x_ref[...]
    for copy in copies[0]:
        copy.wait()
    for cols in tiles(hidden_ref.shape[1]):
        pre_ref[:, cols] = dot(x, gate[:, cols])
    for copy in copies[1] + copies[2]:
        copy.wait()
    for cols in tiles(hidden_ref.shape[1]):
        gate_pre = pre_ref[:, cols]
        up_pre = dot(x, up[:, cols])
        hidden_grad = dot(cot_ref[...], down[:, cols])
        sigma = 1.0 / (1.0 + jnp.exp(-gate_pre))
        silu = gate_pre * sigma
        hidden_ref[:, cols] = (silu * up_pre).astype(bf16)
        gate_grad_ref[:, cols] = (
            hidden_grad * up_pre * sigma * (1.0 + gate_pre * (1.0 - sigma))
        ).astype(bf16)
        up_grad_ref[:, cols] = (hidden_grad * silu).astype(bf16)
    two_grad = lambda at: dot(gate_grad_ref[...], gate[at], NT) + dot(up_grad_ref[...], up[at], NT)
    cut_all(two_grad, own_ref, sends)


def cut_all(product, own_ref, sends):
    count, _, width = own_ref.shape
    group = max(1, 1024 // width)
    for start in range(0, count, group):
        total = product(slice(start * width, (start + group) * width))
        for n in range(group):
            cut(start + n, total[:, n * width : (n + 1) * width], own_ref, sends)


def cut(n, total, own_ref, sends):
    rows = own_ref.shape[1]
    own_ref[n] = total[:rows]
    for j, ref in enumerate(sends):
        ref[n] = total[(j + 1) * rows : (j + 2) * rows].astype(bf16)


def down_kernel(three_ref, all_ref, own_ref, *refs):
    sends, (down, sem) = refs[:-2], refs[-2:]
    hidden_ref = three_ref.at[2]
    for copy in fetch(all_ref, 2, down, sem):
        copy.wait()
    cut_all(lambda at: dot(hidden_ref[...], down[at], NT), own_ref, sends)


def block_out_kernel(mid_ref, own_ref, *refs):
    total = mid_ref[...] + own_ref[...]
    for ref in refs[:-1]:
        total = total + ref[...].astype(f32)
    refs[-1][...] = total.astype(bf16)


def ffn_weights_kernel(place_ref, *refs):
    x, cot, grads, out_ref, both = refs[:2], refs[2:4], refs[4:6], refs[6], refs[7]
    tok, width = x[0].shape[1:]

    @pl.when(pl.program_id(0) == 0)
    def _():
        for c, ref in enumerate(grads):
            both[:, c * tok : (c + 1) * tok, :] = ref[...]

    for i, left in enumerate((x, x, cot)):
        left = jnp.concatenate([left[0][0], left[1][0]], axis=0)
        out_ref[i * width : (i + 1) * width] = dot(left, both[i], TN).astype(bf16)


def norm_back(normal, inv, grad, gain):
    scaled = grad * gain
    inner = row_mean(scaled * normal)
    return inv[None] * (scaled - row_mean(scaled)[None] - normal * inner[None])


def token_sum(x3):
    return jnp.sum(x3, axis=1, keepdims=True)


def mid_back_kernel(cot_ref, mid_ref, gain_ref, own_ref, *refs):
    grad_ref, low_ref, gain_grad_ref, bias_grad_ref = refs[-4:]
    total = own_ref[...]
    for ref in refs[:-4]:
        total = total + ref[...].astype(f32)
    normal, inv = row_stats(mid_ref[...])
    gain_grad_ref[...] = token_sum(total * normal)
    bias_grad_ref[...] = token_sum(total)
    cot = split(cot_ref[...].astype(f32), mid_ref.shape[0])
    grad = cot + norm_back(normal, inv, total, gain_ref[...])
    grad_ref[...] = grad
    low_ref[...] = grad.astype(bf16)


def attend_back_kernel(
    slots, peers, order_ref, at_ref, hide_ref, table_ref, q_ref, here_ref, early_ref, log_ref, *refs
):
    count = order_ref.shape[0]
    lows = refs[:peers]
    weights = refs[peers : peers + count]
    kept_ref, sent_ref, dq_ref, dhere_ref, dearly_ref, datt = refs[peers + count :]
    rows, feat = q_ref.shape
    part = rows // peers
    scale = HD**-0.5
    low = {}
    for ref, which in zip((kept_ref, sent_ref), slots):
        for i, k in enumerate(which):
            low[k] = ref.at[i]
            for j in range(peers):
                at = pl.ds(pl.multiple_of(at_ref[j] * part, part), part)
                ref[i, at, :] = lows[j][order_ref[k]]
    for cols in tiles(feat):
        total = dot(low[0][...], weights[0][cols], NT)
        for k in range(1, count):
            total = total + dot(low[k][...], weights[k][cols], NT)
        datt[:, cols] = total.astype(bf16)
    for pair in range(feat // (2 * HD)):
        cols = slice(pair * 2 * HD, (pair + 1) * 2 * HD)
        q = q_ref[:, cols]
        k = jnp.concatenate([early_ref[0, :, cols], here_ref[0, :, cols]], axis=0)
        v = jnp.concatenate([early_ref[1, :, cols], here_ref[1, :, cols]], axis=0)
        da = datt[:, cols]
        grads = []
        for h in range(2):
            mask = head_mask(rows, h)
            scores = dot(jnp.where(mask, q, 0), k, NT) * scale + hide_ref[...]
            probs = jnp.exp(scores - log_ref[2 * pair + h])
            weight_grad = dot(jnp.where(mask, da, 0), v, NT)
            inner = jnp.sum(probs * weight_grad, axis=-1, keepdims=True)
            score_grad = (probs * (weight_grad - inner)).astype(bf16)
            grads.append(
                (
                    dot(score_grad, k) * scale,
                    dot(score_grad, q, TN) * scale,
                    dot(probs.astype(bf16), da, TN),
                )
            )
        dq = jnp.where(head_mask(rows, 0), grads[0][0], grads[1][0])
        dq_ref[:, cols] = spin(dq, table_ref[...], -1).astype(bf16)
        for i in (1, 2):
            both = jnp.where(head_mask(2 * rows, 0), grads[0][i], grads[1][i])
            dearly_ref[i - 1, :, cols] = both[:rows].astype(bf16)
            dhere_ref[i - 1, :, cols] = both[rows:]


def one_grad_kernel(
    order_ref, at_ref, x_ref, table_ref, dq_ref, dhere_ref, dback_ref, *refs
):
    count = order_ref.shape[0]
    weights, refs = refs[:count], refs[count:]
    ffn_gain_ref, ffn_bias_ref, back_ref, small_ref, own_ref = refs[:5]
    sends, part_ref = refs[5:-1], refs[-1]
    width = own_ref.shape[2]
    back_refs = [back_ref.at[j] for j in range(3)]
    back_refs[0][...] = dq_ref[...]
    dk = dhere_ref[0] + dback_ref[0].astype(f32)
    back_refs[1][...] = spin(dk, table_ref[...], -1).astype(bf16)
    back_refs[2][...] = (dhere_ref[1] + dback_ref[1].astype(f32)).astype(bf16)
    row = 4 * count
    for ref in back_refs:
        bias = jnp.sum(ref[...].astype(f32), axis=0, keepdims=True)
        for at in range(0, ref.shape[1], width):
            small_ref[row : row + 1] = bias[:, at : at + width]
            row += 1
    for k, weight in enumerate(weights):
        part_ref[order_ref[k]] = sum(dot(ref[...], weight[j], NT) for j, ref in enumerate(back_refs))
    normal, _ = row_stats(split(x_ref[...].astype(f32), count))
    small_ref[:count] = token_sum(part_ref[...] * normal)[:, 0]
    small_ref[count : 2 * count] = token_sum(part_ref[...])[:, 0]
    small_ref[2 * count : 3 * count] = ffn_gain_ref[:, 0]
    small_ref[3 * count : 4 * count] = ffn_bias_ref[:, 0]
    hand_out(at_ref, part_ref, own_ref, sends)


def attention_weights_kernel(slots, halves, *refs):
    x, back, low, att, outs = refs[:2], refs[2:4], refs[4:6], refs[6:8], refs[8:]
    part = att[0].shape[1] // 2
    for h, both in enumerate(halves):
        cols = slice(h * part, (h + 1) * part)
        for ref, which in zip(outs[2 * h :], both):
            for i, k in enumerate(which):
                at = slots[0].index(k)
                for j in range(4):
                    left = x if j < 3 else low
                    right = [b[j, :, cols] for b in back] if j < 3 else [a[:, cols] for a in att]
                    total = dot(left[0][at], right[0], TN) + dot(left[1][at], right[1], TN)
                    ref[i, j] = total.astype(bf16)


def outputs_kernel(terms, own_ref, other_ref, *refs):
    parts, outs = refs[: 2 * terms], refs[2 * terms :]
    vector_refs, (bias_ref, qkv_ref, out_ref) = outs[:-3], outs[-3:]
    part = qkv_ref.shape[2] // 2
    for h in range(2):
        cols = slice(h * part, (h + 1) * part)
        for j in range(4):
            group = parts[h * terms : (h + 1) * terms]
            total = sum(ref[ref.shape[0] - 1, j].astype(f32) for ref in group)
            if j < 3:
                qkv_ref[j, :, cols] = total
            else:
                out_ref[cols, :] = total.T
    small = own_ref[...] + other_ref[...]
    rows, width = vector_refs[0].shape[0], small.shape[1]
    count = rows * vector_refs[0].shape[1] // width
    per = width // vector_refs[0].shape[1]
    for v, ref in enumerate(vector_refs):
        for n in range(count):
            for i in range(per):
                lanes = slice(i * ref.shape[1], (i + 1) * ref.shape[1])
                row = v * count + n
                ref[n * per + i : n * per + i + 1] = small[row : row + 1, lanes]
    row = len(vector_refs) * count
    for j in range(3):
        for at in range(0, bias_ref.shape[1], width):
            bias_ref[j : j + 1, at : at + width] = small[row : row + 1]
            row += 1


def input_grad_kernel(x_ref, gain_ref, mid_grad_ref, own_ref, small_ref, *refs):
    parts, out_ref = refs[:-1], refs[-1]
    count, rows, width = own_ref.shape
    total = own_ref[...]
    for ref in parts:
        total = total + ref[...].astype(f32)
    normal, inv = row_stats(split(x_ref[...].astype(f32), count))
    grad = mid_grad_ref[...] + norm_back(normal, inv, total, gain_ref[...])
    out_ref[: count * rows] = grad.astype(bf16).reshape(count * rows, width)
    out_ref[count * rows :] = small_ref[: 4 * count].astype(bf16)


def join_kernel(at_ref, *refs):
    out_ref = refs[-1]
    slices, rows, width = refs[0].shape
    for j, ref in enumerate(refs[:-1]):
        at = pl.ds(pl.multiple_of(at_ref[j] * rows, rows), rows)
        for n in range(slices):
            out_ref[at, n * width : (n + 1) * width] = ref[n]


def join_grad_kernel(at_ref, small_ref, *refs):
    blocks, (out_ref, total_ref) = refs[:-2], refs[-2:]
    width = small_ref.shape[1]
    count = out_ref.shape[1] // width
    rows = out_ref.shape[0] // len(blocks)
    total_ref[...] = small_ref[...]
    for j, ref in enumerate(blocks):
        at = pl.ds(pl.multiple_of(at_ref[j] * rows, rows), rows)
        for n in range(count):
            out_ref[at, n * width : (n + 1) * width] = ref[n * rows : (n + 1) * rows]
        if j:
            total_ref[: 4 * count] += ref[count * rows :].astype(f32)


def on_device(
    block_in,
    seq_lengths,
    attn_gain,
    attn_bias,
    qkv_weight,
    qkv_bias,
    out_weight,
    ffn_gain,
    ffn_bias,
    gate_up_weight,
    down_weight,
    out_cotangent,
):
    tok, model = block_in.shape
    feat = qkv_weight.shape[2]
    hid = down_weight.shape[0]
    plane = Plane()
    count = plane.count
    width = model // count
    peers = lax.axis_size("tensor")
    chunk = tok // peers
    heads = feat // HD
    order = plane.me ^ jnp.arange(count, dtype=jnp.int32)
    at = lax.axis_index("tensor") ^ jnp.arange(peers, dtype=jnp.int32)

    offset = lax.axis_index("context") * tok
    places = offset + jnp.arange(tok, dtype=jnp.int32)
    lengths = seq_lengths[0]
    ends = jnp.cumsum(lengths)
    starts = jnp.sum(jnp.where(ends[None, :] <= places[:, None], lengths[None, :], 0), axis=1)
    turn = ROT // 2
    frequency = jnp.exp(jnp.arange(turn).astype(f32) * (-2.0 * math.log(10000.0) / ROT))
    angles = (places - starts).astype(f32)[:, None] * frequency[None, :]
    cosine = jnp.tile(jnp.cos(angles), (1, 128 // turn))
    sine = jnp.tile(jnp.sin(angles), (1, 128 // turn))
    lane = jnp.arange(128)[None, :] % HD
    tables = jnp.stack(
        [
            jnp.where(lane < ROT, cosine, 1.0),
            jnp.where(lane < turn, -sine, 0.0),
            jnp.where((lane >= turn) & (lane < ROT), sine, 0.0),
        ]
    )
    key_places = offset - tok + jnp.arange(2 * tok, dtype=jnp.int32)
    visible = (key_places[None, :] <= places[:, None]) & (key_places[None, :] >= starts[:, None])
    hide = jnp.where(visible, 0.0, NEG).astype(f32)

    by_slice = lambda vec: vec.reshape(count, 1, width)
    slots = (plane.kept, plane.sent)
    slice_pair = (shape((count // 2, tok, width), bf16),) * 2
    slices = pltpu.VMEM((count, tok, width), bf16)
    one_flat, one_kept, one_sent, in_chunk = call(
        functools.partial(norm_kernel, slots), "norm_one",
        (shape((tok, model), bf16), *slice_pair, shape((chunk, model), bf16)),
        (order, at, block_in, by_slice(attn_gain), by_slice(attn_bias)), [SM, SM] + [VM] * 3,
        scratch=[slices],
    )
    cot, cot_kept, cot_sent, cot_chunk = call(
        functools.partial(reorder_kernel, slots), "cotangent_rows",
        (shape((tok, model), bf16), *slice_pair, shape((chunk, model), bf16)), (order, at, out_cotangent), [SM, SM, VM],
        scratch=[slices],
    )

    bias_rows = qkv_bias.reshape(3, 1, feat)
    ffn_shard = call(
        pack_kernel, "ffn_shard", shape((3 * width, hid), bf16),
        (gate_up_weight, down_weight), [VM, VM],
    )
    qkv_slots = plane.gather(qkv_weight, ffn_shard, one_flat, bias_rows, tables, hide)
    qkv_list = [qkv_slots[k] for k in range(count)]
    out_near = plane.near(tie(out_weight, ffn_shard))
    first = (qkv_slots[plane.up[0]], qkv_slots[plane.up[-1]])
    ffn_all = lax.all_gather(tie(ffn_shard, first), PLANE, axis=0, tiled=False)

    queries, here = call(
        qkv_kernel, "qkv", (shape((tok, feat), bf16), shape((2, tok, feat), bf16)),
        (one_flat, bias_rows, tables, *qkv_list), [VM] * (3 + count),
    )
    early = lax.ppermute(here, "context", [(i, i + 1) for i in range(plane.context - 1)])
    out_slots = plane.pass_on(out_near, queries)
    out_list = [out_slots[k] for k in range(count)]
    sends = [shape((count, chunk, width), bf16)] * (peers - 1)
    own_shape = shape((count, chunk, width), f32)
    attended, logs, own, *parts = call(
        functools.partial(attend_kernel, count), "attend",
        (shape((tok, feat), bf16), shape((heads, tok, 1), f32), own_shape, *sends),
        (order, at, hide, queries, here, early, *out_list),
        [SM, SM] + [VM] * (4 + count),
        scratch=[pltpu.VMEM((count, tok, width), f32)],
    )
    got = tensor_exchange([None] + parts)
    cot_got, one_got, att_got = plane.across((cot_sent, one_sent, attended))
    own = tie(own, cot_got, one_got, att_got)
    mid, normed_chunk = call(
        mid_kernel, "mid", (own_shape, sends[0]),
        (in_chunk, by_slice(ffn_gain), by_slice(ffn_bias), own, *got), [VM] * (4 + len(got)),
    )
    normed_two = tensor_gather(normed_chunk)

    buffer = pltpu.VMEM((model, hid), bf16)
    two_kept, two_sent, three, grad_own, *grad_parts = call(
        functools.partial(ffn_kernel, slots, peers), "ffn",
        (*slice_pair, shape((3, tok, hid), bf16), own_shape, *sends),
        (order, *normed_two, cot, ffn_all), [SM] + [VM] * (peers + 1) + [HB],
        scratch=[buffer] * 3
        + [
            pltpu.SemaphoreType.DMA((3, count)), pltpu.VMEM((tok, model), bf16),
            pltpu.VMEM((tok, hid), f32),
        ],
    )
    got = tensor_exchange([None] + grad_parts)
    two_got, three_got = plane.across((two_sent, three))
    place = jnp.stack([plane.rank(k) for k in plane.kept])
    of_slot = pl.BlockSpec((1, tok, width), lambda i, place: (i, 0, 0))
    whole = pl.BlockSpec((3, tok, hid), lambda i, place: (0, 0, 0))
    ffn_grads = pl.pallas_call(
        ffn_weights_kernel,
        grid_spec=pltpu.PrefetchScalarGridSpec(
            num_scalar_prefetch=1,
            grid=(count // 2,),
            in_specs=[of_slot] * 4 + [whole] * 2,
            out_specs=pl.BlockSpec((3 * width, hid), lambda i, place: (place[i], 0)),
            scratch_shapes=[pltpu.VMEM((3, 2 * tok, hid), bf16)],
        ),
        out_shape=shape((count // 2 * 3 * width, hid), bf16),
        **params("ffn_weights"),
    )(place, two_kept, two_got, cot_kept, cot_got, three, three_got)
    ffn_total = lax.psum_scatter(
        ffn_grads, PLANE, scatter_dimension=0, axis_index_groups=plane.groups, tiled=True
    )
    grad_own = tie(grad_own, ffn_grads)
    vec = shape((count, 1, width), f32)
    mid_grad, low_chunk, ffn_gain_grad, ffn_bias_grad = call(
        mid_back_kernel, "mid_back", (own_shape, sends[0], vec, vec),
        (cot_chunk, mid, by_slice(ffn_gain), grad_own, *got), [VM] * (4 + len(got)),
    )
    low_blocks = tensor_gather(low_chunk)
    down_own, *down_parts = call(
        down_kernel, "down", (own_shape, *sends), (tie(three, low_chunk), ffn_all), [VM, HB],
        scratch=[buffer, pltpu.SemaphoreType.DMA((count,))],
    )
    down_got = tensor_exchange([None, *tie(down_parts, low_blocks)])
    out_chunk = call(
        block_out_kernel, "block_out", sends[0], (mid, down_own, *down_got),
        [VM] * (2 + len(down_got)),
    )
    out_blocks = tensor_gather(out_chunk)

    low_kept, low_sent, dq, dhere, dearly = call(
        functools.partial(attend_back_kernel, slots, peers), "attend_back",
        (
            *slice_pair, shape((tok, feat), bf16),
            shape((2, tok, feat), f32), shape((2, tok, feat), bf16),
        ),
        (order, at, hide, tables, queries, here, early, logs, *low_blocks, *out_list),
        [SM, SM] + [VM] * (6 + peers + count),
        scratch=[pltpu.VMEM((tok, feat), bf16)],
    )
    low_got = plane.across(low_sent)
    dback = lax.ppermute(dearly, "context", [(i + 1, i) for i in range(plane.context - 1)])
    small_shape = shape((4 * count + 3 * feat // width, width), f32)
    back, small, own, *parts = call(
        one_grad_kernel, "one_grad",
        (
            shape((3, tok, feat), bf16), small_shape, own_shape, *sends,
        ),
        (
            order, at, block_in, tables, dq, tie(dhere, out_blocks, low_got), dback, *qkv_list,
            ffn_gain_grad, ffn_bias_grad,
        ),
        [SM, SM] + [VM] * (7 + count),
        scratch=[pltpu.VMEM((count, tok, width), f32)],
    )
    got = tensor_exchange([None, *parts])
    halves = (plane.halves(plane.down), plane.halves(plane.up))
    back_got = plane.across(back)
    small = plane.chip_total(small)
    weight_grads = call(
        functools.partial(attention_weights_kernel, slots, halves), "attention_weights",
        (shape((count // 4, 4, width, feat // 2), bf16),) * 4,
        (one_kept, one_got, tie(back, small), back_got, low_kept, low_got, attended, att_got), [VM] * 8,
    )
    terms_a = scatter(plane, *weight_grads[:2], plane.down)
    terms_b = scatter(plane, *weight_grads[2:], plane.up)
    grad_chunk = call(
        input_grad_kernel, "input_grad", shape((count * chunk + 4 * count, width), bf16),
        (in_chunk, by_slice(attn_gain), mid_grad, own, small, *got), [VM] * (5 + len(got)),
    )
    grad_blocks = tensor_gather(grad_chunk)
    gate_up_grad, down_grad = call(
        ffn_out_kernel, "ffn_out", (shape((2, width, hid), f32), shape((hid, width), f32)),
        (ffn_total,), [VM],
    )
    block_out = call(
        join_kernel, "block_out_rows", shape((tok, model), bf16), (at, *out_blocks),
        [SM] + [VM] * peers,
    )
    input_grad, small = call(
        join_grad_kernel, "input_grad_rows", (shape((tok, model), bf16), small_shape),
        (at, small, *tie(grad_blocks, block_out, down_grad)), [SM] + [VM] * (1 + peers),
    )

    terms = (*terms_a, *terms_b)
    lanes = min(width, 128)
    *vectors, bias_grad, qkv_grad, out_grad = call(
        functools.partial(outputs_kernel, len(terms_a)), "outputs",
        (
            *[shape((model // lanes, lanes), f32)] * 4, shape((3, feat), f32),
            shape((3, width, feat), f32), shape((feat, width), f32),
        ),
        (small, plane.across(small), *terms), [VM] * (2 + len(terms)),
    )
    vectors = [v.reshape(model) for v in vectors]
    return (
        block_out,
        input_grad,
        vectors[0],
        vectors[1],
        qkv_grad,
        bias_grad,
        out_grad,
        vectors[2],
        vectors[3],
        gate_up_grad,
        down_grad,
    )


def solution(mesh):
    in_specs = (
        P(("fsdp", "context"), None),
        P("fsdp", None),
        P(),
        P(),
        P(None, ("fsdp", "context"), "tensor"),
        P(None, "tensor"),
        P("tensor", ("fsdp", "context")),
        P(),
        P(),
        P(None, ("fsdp", "context"), "tensor"),
        P("tensor", ("fsdp", "context")),
        P(("fsdp", "context"), None),
    )
    out_specs = (
        P(("fsdp", "context"), None),
        P(("fsdp", "context"), None),
        P(),
        P(),
        P(None, ("fsdp", "context"), "tensor"),
        P(None, "tensor"),
        P("tensor", ("fsdp", "context")),
        P(),
        P(),
        P(None, ("fsdp", "context"), "tensor"),
        P("tensor", ("fsdp", "context")),
    )
    return jax.shard_map(
        on_device, mesh=mesh, in_specs=in_specs, out_specs=out_specs, check_vma=False
    )
```

```python
import functools
import math

import jax
import jax.numpy as jnp
from jax import lax
from jax.experimental import pallas as pl
from jax.experimental.pallas import tpu as pltpu
from jax.sharding import PartitionSpec as P

HD = 64
ROT = 16
EPS = 1e-05
NEG = -1e30
f32 = jnp.float32
bf16 = jnp.bfloat16
VM = pl.BlockSpec(memory_space=pltpu.VMEM)
SM = pl.BlockSpec(memory_space=pltpu.SMEM)
HB = pl.BlockSpec(memory_space=pl.ANY)
PLANE = ("fsdp", "context")


def shape(dims, dtype):
    return jax.ShapeDtypeStruct(tuple(dims), dtype)


WEIGHT = dict(
    norm_one=5, cotangent_rows=5, qkv=10, mid=250, mid_back=60, attend_back=200, block_out=5,
    input_grad=8, input_grad_rows=8,
)


VMEM = dict(one_grad=32, attention_weights=24, input_grad=24, input_grad_rows=24, outputs=24)


def params(name):
    return dict(
        name=name,
        compiler_params=pltpu.CompilerParams(vmem_limit_bytes=VMEM.get(name, 56) * 2**20),
        cost_estimate=pl.CostEstimate(
            flops=int(1.15e9 * WEIGHT.get(name, 0)), bytes_accessed=0, transcendentals=0
        ),
    )


def call(kernel, name, outs, args, specs, scratch=()):
    return pl.pallas_call(
        kernel,
        out_shape=outs,
        in_specs=specs,
        out_specs=jax.tree.map(lambda _: VM, outs),
        scratch_shapes=list(scratch),
        **params(name),
    )(*args)


def dot(a, b, dims=((1,), (0,))):
    return lax.dot_general(a, b, (dims, ((), ())), preferred_element_type=f32)


NT = ((1,), (1,))
TN = ((0,), (0,))


def tie(value, *others):
    return lax.optimization_barrier((value, others))[0]


class Plane:
    def __init__(self):
        self.fsdp = lax.axis_size("fsdp")
        self.context = lax.axis_size("context")
        self.count = self.fsdp * self.context
        self.me = lax.axis_index("fsdp") * self.context + lax.axis_index("context")
        self.core = self.context
        bits = [1 << i for i in range(int(math.log2(self.count))) if (1 << i) != self.core]
        self.up, self.down = bits, bits[::-1]
        self.kept = [k for k in range(self.count) if not k & self.core]
        self.sent = [k ^ self.core for k in self.kept]
        own = [[d for d in range(self.count) if d & self.core == c] for c in (0, self.core)]
        self.groups = own

    def rank(self, k):
        low = self.core - 1
        squeeze = lambda d: (d & low) | ((d >> 1) & ~low)
        return squeeze(self.me) ^ squeeze(k)

    def swap(self, value, mask):
        pairs = [(i, i ^ mask) for i in range(self.count)]
        return lax.ppermute(value, ("fsdp", "context"), pairs)

    def across(self, value):
        return jax.tree.map(lambda v: self.swap(v, self.core), value)

    def gather(self, shard, *after):
        slots = {k: self.swap(shard, k) if k else shard for k in self.kept}
        for k in self.kept:
            value = tie(slots[k], after) if after and k == self.kept[-1] else slots[k]
            slots[k ^ self.core] = self.across(value)
        return slots

    def near(self, shard):
        return {0: shard} | {bit: self.swap(shard, bit) for bit in self.up}

    def pass_on(self, slots, *after):
        first = tie(slots[self.up[0]], after)
        slots = dict(slots)
        for k in self.kept:
            if k not in slots:
                source = k & -k
                value = first if source == self.up[0] else slots[source]
                slots[k] = self.swap(value, k ^ source)
        return slots | {k ^ self.core: self.across(v) for k, v in slots.items()}

    def halves(self, order):
        slots = sorted(self.kept, key=lambda k: tuple(not k & bit for bit in order))
        return slots[: len(slots) // 2], slots[len(slots) // 2 :]

    def chip_total(self, value):
        for bit in self.up:
            value = value + self.swap(value, bit)
        return value


def scatter(plane, first, second, order):
    low, terms = first, [second]
    for bit in order:
        terms.append(plane.swap(low, bit))
        rest = terms[-1].shape[0] // 2
        if rest:
            pick = lambda t: t[t.shape[0] - 2 * rest :][:rest].astype(f32)
            low = sum(pick(t) for t in terms).astype(bf16)
    return terms


def tensor_swap(value, j):
    peers = lax.axis_size("tensor")
    return lax.ppermute(value, "tensor", [(i, i ^ j) for i in range(peers)])


def tensor_exchange(parts):
    return [tensor_swap(part, j) for j, part in enumerate(parts) if j]


def tensor_gather(part):
    return [part] + [tensor_swap(part, j) for j in range(1, lax.axis_size("tensor"))]


def row_stats(x3):
    size = x3.shape[0] * x3.shape[2]
    mean = jnp.sum(jnp.sum(x3, axis=0), axis=-1, keepdims=True) / size
    center = x3 - mean[None]
    var = jnp.sum(jnp.sum(center * center, axis=0), axis=-1, keepdims=True) / size
    inv = lax.rsqrt(var + EPS)
    return center * inv[None], inv


def row_mean(x3):
    return jnp.sum(jnp.sum(x3, axis=0), axis=-1, keepdims=True) / (x3.shape[0] * x3.shape[2])


def split(x, count):
    width = x.shape[1] // count
    return jnp.stack([x[:, i * width : (i + 1) * width] for i in range(count)])


def by_slot(slots, order_ref, from_ref, kept_ref, sent_ref):
    for ref, which in zip((kept_ref, sent_ref), slots):
        for i, k in enumerate(which):
            ref[i] = from_ref[order_ref[k]]


def norm_kernel(
    slots, order_ref, at_ref, x_ref, gain_ref, bias_ref, flat_ref, kept_ref, sent_ref, chunk_ref, normed
):
    count, _, width = normed.shape
    rows = chunk_ref.shape[0]
    chunk_ref[...] = x_ref[pl.ds(pl.multiple_of(at_ref[0] * rows, rows), rows), :]
    normal, _ = row_stats(split(x_ref[...].astype(f32), count))
    normed[...] = (normal * gain_ref[...] + bias_ref[...]).astype(bf16)
    by_slot(slots, order_ref, normed, kept_ref, sent_ref)
    for k in range(count):
        flat_ref[:, k * width : (k + 1) * width] = normed[order_ref[k]]


def reorder_kernel(slots, order_ref, at_ref, x_ref, out_ref, kept_ref, sent_ref, chunk_ref, slices):
    rows = x_ref.shape[0] // at_ref.shape[0]
    chunk_ref[...] = x_ref[pl.ds(pl.multiple_of(at_ref[0] * rows, rows), rows), :]
    for j in range(at_ref.shape[0]):
        block = x_ref[pl.ds(pl.multiple_of(at_ref[j] * rows, rows), rows), :]
        out_ref[j * rows : (j + 1) * rows, :] = block
        slices[:, j * rows : (j + 1) * rows, :] = split(block, slices.shape[0])
    by_slot(slots, order_ref, slices, kept_ref, sent_ref)


def spin(x, tables, sign):
    parts = []
    for i in range(x.shape[1] // 128):
        v = x[:, i * 128 : (i + 1) * 128]
        turned = pltpu.roll(v, 128 - ROT // 2, 1) * tables[1] + pltpu.roll(v, ROT // 2, 1) * tables[2]
        parts.append(v * tables[0] + (turned if sign > 0 else -turned))
    return jnp.concatenate(parts, axis=1)


def qkv_kernel(x_ref, bias_ref, table_ref, *refs):
    weights, (q_ref, kv_ref) = refs[:-2], refs[-2:]
    feat, width = q_ref.shape[1], weights[0].shape[1]
    for cols in tiles(feat):
        for j in range(3):
            total = bias_ref[j, :, cols]
            for k, weight in enumerate(weights):
                total = total + dot(x_ref[:, k * width : (k + 1) * width], weight[j, :, cols])
            if j < 2:
                total = spin(total, table_ref[...], 1)
            if j == 0:
                q_ref[:, cols] = total.astype(bf16)
            else:
                kv_ref[j - 1, :, cols] = total.astype(bf16)


def head_mask(rows, h):
    lane = lax.broadcasted_iota(jnp.int32, (rows, 2 * HD), 1)
    return (lane // HD) == h


def attend_kernel(count, order_ref, at_ref, hide_ref, q_ref, here_ref, early_ref, *refs):
    weights = refs[:count]
    att_ref, log_ref, own_ref = refs[count : count + 3]
    sends = refs[count + 3 : -1]
    part_ref = refs[-1]
    rows, feat = q_ref.shape
    scale = HD**-0.5
    for pair in range(feat // (2 * HD)):
        cols = slice(pair * 2 * HD, (pair + 1) * 2 * HD)
        q = q_ref[:, cols] * scale
        out = []
        for h in range(2):
            mine = jnp.where(head_mask(rows, h), q, 0)
            first = dot(mine, early_ref[0, :, cols], NT) + hide_ref[:, :rows]
            second = dot(mine, here_ref[0, :, cols], NT) + hide_ref[:, rows:]
            top = jnp.max(jnp.maximum(first, second), axis=-1, keepdims=True)
            first, second = jnp.exp(first - top), jnp.exp(second - top)
            total = jnp.sum(first + second, axis=-1, keepdims=True)
            log_ref[2 * pair + h] = top + jnp.log(total)
            mixed = dot(first.astype(bf16), early_ref[1, :, cols])
            mixed = mixed + dot(second.astype(bf16), here_ref[1, :, cols])
            out.append(mixed * (1.0 / total))
        att_ref[:, cols] = jnp.where(head_mask(rows, 0), out[0], out[1]).astype(bf16)
    for k in range(count):
        part_ref[order_ref[k]] = dot(att_ref[...], weights[k][...])
    hand_out(at_ref, part_ref, own_ref, sends)


def hand_out(at_ref, part_ref, own_ref, sends):
    rows = own_ref.shape[1]
    for j in range(at_ref.shape[0]):
        block = part_ref[:, pl.ds(pl.multiple_of(at_ref[j] * rows, rows), rows), :]
        if j == 0:
            own_ref[...] = block
        else:
            sends[j - 1][...] = block.astype(bf16)


def ffn_out_kernel(total_ref, gate_up_ref, down_ref):
    width = down_ref.shape[1]
    for i in range(2):
        gate_up_ref[i] = total_ref[i * width : (i + 1) * width].astype(f32)
    down_ref[...] = total_ref[2 * width :].astype(f32).T


def mid_kernel(x_ref, gain_ref, bias_ref, own_ref, *refs):
    mid_ref, normed_ref = refs[-2:]
    total = own_ref[...]
    for ref in refs[:-2]:
        total = total + ref[...].astype(f32)
    mid = split(x_ref[...].astype(f32), own_ref.shape[0]) + total
    mid_ref[...] = mid
    normal, _ = row_stats(mid)
    normed_ref[...] = (normal * gain_ref[...] + bias_ref[...]).astype(bf16)


def pack_kernel(gate_up_ref, down_ref, out_ref):
    width = down_ref.shape[1]
    out_ref[:width] = gate_up_ref[0]
    out_ref[width : 2 * width] = gate_up_ref[1]
    out_ref[2 * width :] = down_ref[...].T


def fetch(all_ref, which, to_ref, sem):
    count, rows, _ = all_ref.shape
    width = rows // 3
    copies = [
        pltpu.make_async_copy(
            all_ref.at[n, pl.ds(which * width, width)], to_ref.at[pl.ds(n * width, width)], sem.at[n]
        )
        for n in range(count)
    ]
    for copy in copies:
        copy.start()
    return copies


def tiles(size, step=256):
    return [slice(i, min(i + step, size)) for i in range(0, size, step)]


def ffn_kernel(slots, peers, order_ref, *refs):
    blocks = refs[:peers]
    cot_ref, all_ref, kept_ref, sent_ref, three_ref, own_ref = refs[peers : peers + 6]
    gate_grad_ref, up_grad_ref, hidden_ref = (three_ref.at[i] for i in range(3))
    sends, (gate, up, down, sems, x_ref, pre_ref) = refs[peers + 6 : -6], refs[-6:]
    copies = [fetch(all_ref, i, ref, sems.at[i]) for i, ref in enumerate((gate, up, down))]
    rows, width = own_ref.shape[1:]
    for j, ref in enumerate(blocks):
        at = slice(j * rows, (j + 1) * rows)
        for n in range(own_ref.shape[0]):
            x_ref[at, n * width : (n + 1) * width] = ref[n]
        for to_ref, which in zip((kept_ref, sent_ref), slots):
            for i, k in enumerate(which):
                to_ref[i, at, :] = ref[order_ref[k]]
    x = x_ref[...]
    for copy in copies[0]:
        copy.wait()
    for cols in tiles(hidden_ref.shape[1]):
        pre_ref[:, cols] = dot(x, gate[:, cols])
    for copy in copies[1] + copies[2]:
        copy.wait()
    for cols in tiles(hidden_ref.shape[1]):
        gate_pre = pre_ref[:, cols]
        up_pre = dot(x, up[:, cols])
        hidden_grad = dot(cot_ref[...], down[:, cols])
        sigma = 1.0 / (1.0 + jnp.exp(-gate_pre))
        silu = gate_pre * sigma
        hidden_ref[:, cols] = (silu * up_pre).astype(bf16)
        gate_grad_ref[:, cols] = (
            hidden_grad * up_pre * sigma * (1.0 + gate_pre * (1.0 - sigma))
        ).astype(bf16)
        up_grad_ref[:, cols] = (hidden_grad * silu).astype(bf16)
    two_grad = lambda at: dot(gate_grad_ref[...], gate[at], NT) + dot(up_grad_ref[...], up[at], NT)
    cut_all(two_grad, own_ref, sends)


def cut_all(product, own_ref, sends):
    count, _, width = own_ref.shape
    group = max(1, 1024 // width)
    for start in range(0, count, group):
        total = product(slice(start * width, (start + group) * width))
        for n in range(group):
            cut(start + n, total[:, n * width : (n + 1) * width], own_ref, sends)


def cut(n, total, own_ref, sends):
    rows = own_ref.shape[1]
    own_ref[n] = total[:rows]
    for j, ref in enumerate(sends):
        ref[n] = total[(j + 1) * rows : (j + 2) * rows].astype(bf16)


def down_kernel(three_ref, all_ref, own_ref, *refs):
    sends, (down, sem) = refs[:-2], refs[-2:]
    hidden_ref = three_ref.at[2]
    for copy in fetch(all_ref, 2, down, sem):
        copy.wait()
    cut_all(lambda at: dot(hidden_ref[...], down[at], NT), own_ref, sends)


def block_out_kernel(mid_ref, own_ref, *refs):
    total = mid_ref[...] + own_ref[...]
    for ref in refs[:-1]:
        total = total + ref[...].astype(f32)
    refs[-1][...] = total.astype(bf16)


def ffn_weights_kernel(place_ref, *refs):
    x, cot, grads, out_ref, both = refs[:2], refs[2:4], refs[4:6], refs[6], refs[7]
    tok, width = x[0].shape[1:]

    @pl.when(pl.program_id(0) == 0)
    def _():
        for c, ref in enumerate(grads):
            both[:, c * tok : (c + 1) * tok, :] = ref[...]

    for i, left in enumerate((x, x, cot)):
        left = jnp.concatenate([left[0][0], left[1][0]], axis=0)
        out_ref[i * width : (i + 1) * width] = dot(left, both[i], TN).astype(bf16)


def norm_back(normal, inv, grad, gain):
    scaled = grad * gain
    inner = row_mean(scaled * normal)
    return inv[None] * (scaled - row_mean(scaled)[None] - normal * inner[None])


def token_sum(x3):
    return jnp.sum(x3, axis=1, keepdims=True)


def mid_back_kernel(cot_ref, mid_ref, gain_ref, own_ref, *refs):
    grad_ref, low_ref, gain_grad_ref, bias_grad_ref = refs[-4:]
    total = own_ref[...]
    for ref in refs[:-4]:
        total = total + ref[...].astype(f32)
    normal, inv = row_stats(mid_ref[...])
    gain_grad_ref[...] = token_sum(total * normal)
    bias_grad_ref[...] = token_sum(total)
    cot = split(cot_ref[...].astype(f32), mid_ref.shape[0])
    grad = cot + norm_back(normal, inv, total, gain_ref[...])
    grad_ref[...] = grad
    low_ref[...] = grad.astype(bf16)


def attend_back_kernel(
    slots, peers, order_ref, at_ref, hide_ref, table_ref, q_ref, here_ref, early_ref, log_ref, *refs
):
    count = order_ref.shape[0]
    lows = refs[:peers]
    weights = refs[peers : peers + count]
    kept_ref, sent_ref, dq_ref, dhere_ref, dearly_ref, datt = refs[peers + count :]
    rows, feat = q_ref.shape
    part = rows // peers
    scale = HD**-0.5
    low = {}
    for ref, which in zip((kept_ref, sent_ref), slots):
        for i, k in enumerate(which):
            low[k] = ref.at[i]
            for j in range(peers):
                at = pl.ds(pl.multiple_of(at_ref[j] * part, part), part)
                ref[i, at, :] = lows[j][order_ref[k]]
    for cols in tiles(feat):
        total = dot(low[0][...], weights[0][cols], NT)
        for k in range(1, count):
            total = total + dot(low[k][...], weights[k][cols], NT)
        datt[:, cols] = total.astype(bf16)
    for pair in range(feat // (2 * HD)):
        cols = slice(pair * 2 * HD, (pair + 1) * 2 * HD)
        q = q_ref[:, cols]
        k = jnp.concatenate([early_ref[0, :, cols], here_ref[0, :, cols]], axis=0)
        v = jnp.concatenate([early_ref[1, :, cols], here_ref[1, :, cols]], axis=0)
        da = datt[:, cols]
        grads = []
        for h in range(2):
            mask = head_mask(rows, h)
            scores = dot(jnp.where(mask, q, 0), k, NT) * scale + hide_ref[...]
            probs = jnp.exp(scores - log_ref[2 * pair + h])
            weight_grad = dot(jnp.where(mask, da, 0), v, NT)
            inner = jnp.sum(probs * weight_grad, axis=-1, keepdims=True)
            score_grad = (probs * (weight_grad - inner)).astype(bf16)
            grads.append(
                (
                    dot(score_grad, k) * scale,
                    dot(score_grad, q, TN) * scale,
                    dot(probs.astype(bf16), da, TN),
                )
            )
        dq = jnp.where(head_mask(rows, 0), grads[0][0], grads[1][0])
        dq_ref[:, cols] = spin(dq, table_ref[...], -1).astype(bf16)
        for i in (1, 2):
            both = jnp.where(head_mask(2 * rows, 0), grads[0][i], grads[1][i])
            dearly_ref[i - 1, :, cols] = both[:rows].astype(bf16)
            dhere_ref[i - 1, :, cols] = both[rows:]


def one_grad_kernel(
    order_ref, at_ref, x_ref, table_ref, dq_ref, dhere_ref, dback_ref, *refs
):
    count = order_ref.shape[0]
    weights, refs = refs[:count], refs[count:]
    ffn_gain_ref, ffn_bias_ref, back_ref, small_ref, own_ref = refs[:5]
    sends, part_ref = refs[5:-1], refs[-1]
    width = own_ref.shape[2]
    back_refs = [back_ref.at[j] for j in range(3)]
    back_refs[0][...] = dq_ref[...]
    dk = dhere_ref[0] + dback_ref[0].astype(f32)
    back_refs[1][...] = spin(dk, table_ref[...], -1).astype(bf16)
    back_refs[2][...] = (dhere_ref[1] + dback_ref[1].astype(f32)).astype(bf16)
    row = 4 * count
    for ref in back_refs:
        bias = jnp.sum(ref[...].astype(f32), axis=0, keepdims=True)
        for at in range(0, ref.shape[1], width):
            small_ref[row : row + 1] = bias[:, at : at + width]
            row += 1
    for k, weight in enumerate(weights):
        part_ref[order_ref[k]] = sum(dot(ref[...], weight[j], NT) for j, ref in enumerate(back_refs))
    normal, _ = row_stats(split(x_ref[...].astype(f32), count))
    small_ref[:count] = token_sum(part_ref[...] * normal)[:, 0]
    small_ref[count : 2 * count] = token_sum(part_ref[...])[:, 0]
    small_ref[2 * count : 3 * count] = ffn_gain_ref[:, 0]
    small_ref[3 * count : 4 * count] = ffn_bias_ref[:, 0]
    hand_out(at_ref, part_ref, own_ref, sends)


def attention_weights_kernel(slots, halves, *refs):
    x, back, low, att, outs = refs[:2], refs[2:4], refs[4:6], refs[6:8], refs[8:]
    part = att[0].shape[1] // 2
    for h, both in enumerate(halves):
        cols = slice(h * part, (h + 1) * part)
        for ref, which in zip(outs[2 * h :], both):
            for i, k in enumerate(which):
                at = slots[0].index(k)
                for j in range(4):
                    left = x if j < 3 else low
                    right = [b[j, :, cols] for b in back] if j < 3 else [a[:, cols] for a in att]
                    total = dot(left[0][at], right[0], TN) + dot(left[1][at], right[1], TN)
                    ref[i, j] = total.astype(bf16)


def outputs_kernel(terms, own_ref, other_ref, *refs):
    parts, outs = refs[: 2 * terms], refs[2 * terms :]
    vector_refs, (bias_ref, qkv_ref, out_ref) = outs[:-3], outs[-3:]
    part = qkv_ref.shape[2] // 2
    for h in range(2):
        cols = slice(h * part, (h + 1) * part)
        for j in range(4):
            group = parts[h * terms : (h + 1) * terms]
            total = sum(ref[ref.shape[0] - 1, j].astype(f32) for ref in group)
            if j < 3:
                qkv_ref[j, :, cols] = total
            else:
                out_ref[cols, :] = total.T
    small = own_ref[...] + other_ref[...]
    rows, width = vector_refs[0].shape[0], small.shape[1]
    count = rows * vector_refs[0].shape[1] // width
    per = width // vector_refs[0].shape[1]
    for v, ref in enumerate(vector_refs):
        for n in range(count):
            for i in range(per):
                lanes = slice(i * ref.shape[1], (i + 1) * ref.shape[1])
                row = v * count + n
                ref[n * per + i : n * per + i + 1] = small[row : row + 1, lanes]
    row = len(vector_refs) * count
    for j in range(3):
        for at in range(0, bias_ref.shape[1], width):
            bias_ref[j : j + 1, at : at + width] = small[row : row + 1]
            row += 1


def input_grad_kernel(x_ref, gain_ref, mid_grad_ref, own_ref, small_ref, *refs):
    parts, out_ref = refs[:-1], refs[-1]
    count, rows, width = own_ref.shape
    total = own_ref[...]
    for ref in parts:
        total = total + ref[...].astype(f32)
    normal, inv = row_stats(split(x_ref[...].astype(f32), count))
    grad = mid_grad_ref[...] + norm_back(normal, inv, total, gain_ref[...])
    out_ref[: count * rows] = grad.astype(bf16).reshape(count * rows, width)
    out_ref[count * rows :] = small_ref[: 4 * count].astype(bf16)


def join_kernel(at_ref, *refs):
    out_ref = refs[-1]
    slices, rows, width = refs[0].shape
    for j, ref in enumerate(refs[:-1]):
        at = pl.ds(pl.multiple_of(at_ref[j] * rows, rows), rows)
        for n in range(slices):
            out_ref[at, n * width : (n + 1) * width] = ref[n]


def join_grad_kernel(at_ref, small_ref, *refs):
    blocks, (out_ref, total_ref) = refs[:-2], refs[-2:]
    width = small_ref.shape[1]
    count = out_ref.shape[1] // width
    rows = out_ref.shape[0] // len(blocks)
    total_ref[...] = small_ref[...]
    for j, ref in enumerate(blocks):
        at = pl.ds(pl.multiple_of(at_ref[j] * rows, rows), rows)
        for n in range(count):
            out_ref[at, n * width : (n + 1) * width] = ref[n * rows : (n + 1) * rows]
        if j:
            total_ref[: 4 * count] += ref[count * rows :].astype(f32)


def on_device(
    block_in,
    seq_lengths,
    attn_gain,
    attn_bias,
    qkv_weight,
    qkv_bias,
    out_weight,
    ffn_gain,
    ffn_bias,
    gate_up_weight,
    down_weight,
    out_cotangent,
):
    tok, model = block_in.shape
    feat = qkv_weight.shape[2]
    hid = down_weight.shape[0]
    plane = Plane()
    count = plane.count
    width = model // count
    peers = lax.axis_size("tensor")
    chunk = tok // peers
    heads = feat // HD
    order = plane.me ^ jnp.arange(count, dtype=jnp.int32)
    at = lax.axis_index("tensor") ^ jnp.arange(peers, dtype=jnp.int32)

    offset = lax.axis_index("context") * tok
    places = offset + jnp.arange(tok, dtype=jnp.int32)
    lengths = seq_lengths[0]
    ends = jnp.cumsum(lengths)
    starts = jnp.sum(jnp.where(ends[None, :] <= places[:, None], lengths[None, :], 0), axis=1)
    turn = ROT // 2
    frequency = jnp.exp(jnp.arange(turn).astype(f32) * (-2.0 * math.log(10000.0) / ROT))
    angles = (places - starts).astype(f32)[:, None] * frequency[None, :]
    cosine = jnp.tile(jnp.cos(angles), (1, 128 // turn))
    sine = jnp.tile(jnp.sin(angles), (1, 128 // turn))
    lane = jnp.arange(128)[None, :] % HD
    tables = jnp.stack(
        [
            jnp.where(lane < ROT, cosine, 1.0),
            jnp.where(lane < turn, -sine, 0.0),
            jnp.where((lane >= turn) & (lane < ROT), sine, 0.0),
        ]
    )
    key_places = offset - tok + jnp.arange(2 * tok, dtype=jnp.int32)
    visible = (key_places[None, :] <= places[:, None]) & (key_places[None, :] >= starts[:, None])
    hide = jnp.where(visible, 0.0, NEG).astype(f32)

    by_slice = lambda vec: vec.reshape(count, 1, width)
    slots = (plane.kept, plane.sent)
    slice_pair = (shape((count // 2, tok, width), bf16),) * 2
    slices = pltpu.VMEM((count, tok, width), bf16)
    one_flat, one_kept, one_sent, in_chunk = call(
        functools.partial(norm_kernel, slots), "norm_one",
        (shape((tok, model), bf16), *slice_pair, shape((chunk, model), bf16)),
        (order, at, block_in, by_slice(attn_gain), by_slice(attn_bias)), [SM, SM] + [VM] * 3,
        scratch=[slices],
    )
    cot, cot_kept, cot_sent, cot_chunk = call(
        functools.partial(reorder_kernel, slots), "cotangent_rows",
        (shape((tok, model), bf16), *slice_pair, shape((chunk, model), bf16)), (order, at, out_cotangent), [SM, SM, VM],
        scratch=[slices],
    )

    bias_rows = qkv_bias.reshape(3, 1, feat)
    ffn_shard = call(
        pack_kernel, "ffn_shard", shape((3 * width, hid), bf16),
        (gate_up_weight, down_weight), [VM, VM],
    )
    qkv_slots = plane.gather(qkv_weight, ffn_shard, one_flat, bias_rows, tables, hide)
    qkv_list = [qkv_slots[k] for k in range(count)]
    out_near = plane.near(tie(out_weight, ffn_shard))
    first = (qkv_slots[plane.up[0]], qkv_slots[plane.up[-1]])
    ffn_all = lax.all_gather(tie(ffn_shard, first), PLANE, axis=0, tiled=False)

    queries, here = call(
        qkv_kernel, "qkv", (shape((tok, feat), bf16), shape((2, tok, feat), bf16)),
        (one_flat, bias_rows, tables, *qkv_list), [VM] * (3 + count),
    )
    early = lax.ppermute(here, "context", [(i, i + 1) for i in range(plane.context - 1)])
    out_slots = plane.pass_on(out_near, queries)
    out_list = [out_slots[k] for k in range(count)]
    sends = [shape((count, chunk, width), bf16)] * (peers - 1)
    own_shape = shape((count, chunk, width), f32)
    attended, logs, own, *parts = call(
        functools.partial(attend_kernel, count), "attend",
        (shape((tok, feat), bf16), shape((heads, tok, 1), f32), own_shape, *sends),
        (order, at, hide, queries, here, early, *out_list),
        [SM, SM] + [VM] * (4 + count),
        scratch=[pltpu.VMEM((count, tok, width), f32)],
    )
    got = tensor_exchange([None] + parts)
    cot_got, one_got, att_got = plane.across((cot_sent, one_sent, attended))
    own = tie(own, cot_got, one_got, att_got)
    mid, normed_chunk = call(
        mid_kernel, "mid", (own_shape, sends[0]),
        (in_chunk, by_slice(ffn_gain), by_slice(ffn_bias), own, *got), [VM] * (4 + len(got)),
    )
    normed_two = tensor_gather(normed_chunk)

    buffer = pltpu.VMEM((model, hid), bf16)
    two_kept, two_sent, three, grad_own, *grad_parts = call(
        functools.partial(ffn_kernel, slots, peers), "ffn",
        (*slice_pair, shape((3, tok, hid), bf16), own_shape, *sends),
        (order, *normed_two, cot, ffn_all), [SM] + [VM] * (peers + 1) + [HB],
        scratch=[buffer] * 3
        + [
            pltpu.SemaphoreType.DMA((3, count)), pltpu.VMEM((tok, model), bf16),
            pltpu.VMEM((tok, hid), f32),
        ],
    )
    got = tensor_exchange([None] + grad_parts)
    two_got, three_got = plane.across((two_sent, three))
    place = jnp.stack([plane.rank(k) for k in plane.kept])
    of_slot = pl.BlockSpec((1, tok, width), lambda i, place: (i, 0, 0))
    whole = pl.BlockSpec((3, tok, hid), lambda i, place: (0, 0, 0))
    ffn_grads = pl.pallas_call(
        ffn_weights_kernel,
        grid_spec=pltpu.PrefetchScalarGridSpec(
            num_scalar_prefetch=1,
            grid=(count // 2,),
            in_specs=[of_slot] * 4 + [whole] * 2,
            out_specs=pl.BlockSpec((3 * width, hid), lambda i, place: (place[i], 0)),
            scratch_shapes=[pltpu.VMEM((3, 2 * tok, hid), bf16)],
        ),
        out_shape=shape((count // 2 * 3 * width, hid), bf16),
        **params("ffn_weights"),
    )(place, two_kept, two_got, cot_kept, cot_got, three, three_got)
    ffn_total = lax.psum_scatter(
        ffn_grads, PLANE, scatter_dimension=0, axis_index_groups=plane.groups, tiled=True
    )
    grad_own = tie(grad_own, ffn_grads)
    vec = shape((count, 1, width), f32)
    mid_grad, low_chunk, ffn_gain_grad, ffn_bias_grad = call(
        mid_back_kernel, "mid_back", (own_shape, sends[0], vec, vec),
        (cot_chunk, mid, by_slice(ffn_gain), grad_own, *got), [VM] * (4 + len(got)),
    )
    low_blocks = tensor_gather(low_chunk)
    down_own, *down_parts = call(
        down_kernel, "down", (own_shape, *sends), (tie(three, low_chunk), ffn_all), [VM, HB],
        scratch=[buffer, pltpu.SemaphoreType.DMA((count,))],
    )
    down_got = tensor_exchange([None, *tie(down_parts, low_blocks)])
    out_chunk = call(
        block_out_kernel, "block_out", sends[0], (mid, down_own, *down_got),
        [VM] * (2 + len(down_got)),
    )
    out_blocks = [out_chunk] + [tensor_swap(out_chunk, j) for j in range(1, peers - 1)]

    low_kept, low_sent, dq, dhere, dearly = call(
        functools.partial(attend_back_kernel, slots, peers), "attend_back",
        (
            *slice_pair, shape((tok, feat), bf16),
            shape((2, tok, feat), f32), shape((2, tok, feat), bf16),
        ),
        (order, at, hide, tables, queries, here, early, logs, *low_blocks, *out_list),
        [SM, SM] + [VM] * (6 + peers + count),
        scratch=[pltpu.VMEM((tok, feat), bf16)],
    )
    low_got = plane.across(low_sent)
    dback = lax.ppermute(dearly, "context", [(i + 1, i) for i in range(plane.context - 1)])
    small_shape = shape((4 * count + 3 * feat // width, width), f32)
    back, small, own, *parts = call(
        one_grad_kernel, "one_grad",
        (
            shape((3, tok, feat), bf16), small_shape, own_shape, *sends,
        ),
        (
            order, at, block_in, tables, dq, tie(dhere, tuple(out_blocks), low_got), dback, *qkv_list,
            ffn_gain_grad, ffn_bias_grad,
        ),
        [SM, SM] + [VM] * (7 + count),
        scratch=[pltpu.VMEM((count, tok, width), f32)],
    )
    got = tensor_exchange([None, *parts])
    halves = (plane.halves(plane.down), plane.halves(plane.up))
    back_got = plane.across(back)
    small = plane.chip_total(small)
    weight_grads = call(
        functools.partial(attention_weights_kernel, slots, halves), "attention_weights",
        (shape((count // 4, 4, width, feat // 2), bf16),) * 4,
        (one_kept, one_got, tie(back, small), back_got, low_kept, low_got, attended, att_got), [VM] * 8,
    )
    terms_a = scatter(plane, *weight_grads[:2], plane.down)
    terms_b = scatter(plane, *weight_grads[2:], plane.up)
    grad_chunk = call(
        input_grad_kernel, "input_grad", shape((count * chunk + 4 * count, width), bf16),
        (in_chunk, by_slice(attn_gain), mid_grad, own, small, *got), [VM] * (5 + len(got)),
    )
    grad_blocks = tensor_gather(grad_chunk)
    gate_up_grad, down_grad = call(
        ffn_out_kernel, "ffn_out", (shape((2, width, hid), f32), shape((hid, width), f32)),
        (ffn_total,), [VM],
    )
    out_blocks.append(tensor_swap(tie(out_chunk, grad_blocks[1]), peers - 1))
    block_out = call(
        join_kernel, "block_out_rows", shape((tok, model), bf16), (at, *out_blocks),
        [SM] + [VM] * peers,
    )
    input_grad, small = call(
        join_grad_kernel, "input_grad_rows", (shape((tok, model), bf16), small_shape),
        (at, small, *tie(grad_blocks, down_grad)), [SM] + [VM] * (1 + peers),
    )

    terms = (*terms_a, *terms_b)
    lanes = min(width, 128)
    *vectors, bias_grad, qkv_grad, out_grad = call(
        functools.partial(outputs_kernel, len(terms_a)), "outputs",
        (
            *[shape((model // lanes, lanes), f32)] * 4, shape((3, feat), f32),
            shape((3, width, feat), f32), shape((feat, width), f32),
        ),
        (small, plane.across(small), *terms), [VM] * (2 + len(terms)),
    )
    vectors = [v.reshape(model) for v in vectors]
    return (
        block_out,
        input_grad,
        vectors[0],
        vectors[1],
        qkv_grad,
        bias_grad,
        out_grad,
        vectors[2],
        vectors[3],
        gate_up_grad,
        down_grad,
    )


def solution(mesh):
    in_specs = (
        P(("fsdp", "context"), None),
        P("fsdp", None),
        P(),
        P(),
        P(None, ("fsdp", "context"), "tensor"),
        P(None, "tensor"),
        P("tensor", ("fsdp", "context")),
        P(),
        P(),
        P(None, ("fsdp", "context"), "tensor"),
        P("tensor", ("fsdp", "context")),
        P(("fsdp", "context"), None),
    )
    out_specs = (
        P(("fsdp", "context"), None),
        P(("fsdp", "context"), None),
        P(),
        P(),
        P(None, ("fsdp", "context"), "tensor"),
        P(None, "tensor"),
        P("tensor", ("fsdp", "context")),
        P(),
        P(),
        P(None, ("fsdp", "context"), "tensor"),
        P("tensor", ("fsdp", "context")),
    )
    return jax.shard_map(
        on_device, mesh=mesh, in_specs=in_specs, out_specs=out_specs, check_vma=False
    )
```
